256 devices in a mesh: seq: 64 (over y, z_lo, x, core), tp: 4 (over z_hi).
Axes of the slice: x: 4, y: 4, z: 8 (z_hi: 4, z_lo: 2; z = z_hi * 2 + z_lo), core: 2. Of those that a mesh axis runs over, the one named last changes fastest.
Arguments:
- tokens: bfloat16 [256, 64, 1152], P(None, 'seq'), may hold values from -6 to 6
- grad_out: bfloat16 [256, 64, 1152], P('seq'), may hold values from -6 to 6
- qkv_weight: bfloat16 [2, 1152, 3, 1152], P(None, None, None, 'tp'), may hold values from -1 to 1
- out_weight: bfloat16 [2, 1152, 1152], P(None, 'tp'), may hold values from -0.1875 to 0.1875
- mod_shift: float32 [2, 1152], replicated, may hold values from -3 to 3
- mod_scale: float32 [2, 1152], replicated, may hold values from -1.8 to 1.8
- mod_gate: float32 [2, 1152], replicated, may hold values from 0.5 to 1.5
Outputs:
- result: bfloat16 [256, 64, 1152], P('seq')
- grad_in: bfloat16 [256, 64, 1152], P(None, 'seq')
The draws below stay inside these ranges and needn't reach their ends.
All inputs are finite; a program needn't handle non-finite values.
Results may differ from the reference program's by a relative error of at most 0.035.
Values may be sent and summed in bfloat16 or wider, within the bound.
No kernel may reach another device: no remote copies, remote signals or barrier semaphores. Data moves between devices by JAX's collectives and lax.ppermute only.
A program may use at most 64 MiB of HBM per device.

```python
import math
import jax
import jax.numpy as jnp
from jax import lax

HEADS = 16
HEAD_DIM = 72
D = 1152
P_SIZE = 256
FRAMES = 64
N_TP = 4


def draw_qkv_weight(key, part):
    key = jax.random.fold_in(key, 11)
    first = jax.random.fold_in(key, 0)
    base = jax.random.normal(first, (2, D, 3, D), jnp.float32) * D ** (-0.5)
    return jnp.clip(base, -1.0, 1.0).astype(jnp.bfloat16)


def steps_of(own_key, dims, cuts, smallest, top_value):
    loudness, own = 1.0, jax.random.fold_in(own_key, 6)
    for axis_at, parts in cuts:
        draws = jnp.exp(jax.random.uniform(jax.random.fold_in(own, axis_at), (parts,), jnp.float32, smallest / len(cuts), top_value / len(cuts)))
        loudness = loudness * jnp.repeat(draws, dims[axis_at] // parts).reshape([-1 if axis == axis_at else 1 for axis in range(len(dims))])
    return loudness


def scatter_about(own_key, extent, width, bound, cuts=(), dtype=jnp.bfloat16):
    entries = jax.random.normal(own_key, extent, jnp.float32) * width
    if len(cuts) > 0:
        entries = steps_of(own_key, extent, cuts, -0.22, 0.18) * entries
    return jnp.clip(entries, min=-bound, max=bound).astype(dtype)


def setup_inputs(seed: int = 0) -> dict:
    key_of = jax.random.split(jax.random.key(seed), 8)
    return {
        "tokens": scatter_about(key_of[0], (P_SIZE, FRAMES, D), 1.0, 6.0, ((1, 64),)),
        "grad_out": scatter_about(key_of[1], (P_SIZE, FRAMES, D), 1.0, 6.0, ((0, 64),)),
        "qkv_weight": draw_qkv_weight(jax.random.fold_in(key_of[7], 71), 0),
        "out_weight": scatter_about(key_of[3], (2, D, D), D ** -0.5, 0.1875, ((1, 4),)),
        "mod_shift": scatter_about(key_of[4], (2, D), 0.5, 3.0, (), jnp.float32),
        "mod_scale": scatter_about(key_of[5], (2, D), 0.3, 1.8, (), jnp.float32),
        "mod_gate": jnp.clip(jax.random.uniform(key_of[6], (2, D), jnp.float32, 0.5, 1.5), 0.5, 1.5),
    }


def rounded(value):
    return lax.optimization_barrier(value.astype(jnp.bfloat16))

def normalize(tokens, shift_row, scale_row):
    widened = tokens.astype(jnp.float32)
    center = widened - lax.optimization_barrier(jnp.mean(widened, axis=-1, keepdims=True))
    inv_std = lax.rsqrt(lax.optimization_barrier(jnp.mean(center * center, axis=-1, keepdims=True)) + 1e-06)
    normed = center * inv_std
    modded = rounded(normed * (1.0 + scale_row) + shift_row)
    return (modded, normed, inv_std)

def sequence_probs(queries, key_heads):
    scores = jnp.einsum('lhe,mhe->hlm', queries.astype(jnp.float32), key_heads.astype(jnp.float32)) / math.sqrt(HEAD_DIM)
    probs_high = jax.nn.softmax(scores, axis=-1)
    return (probs_high, rounded(probs_high))

def sequence_forward(group_in):
    queries, key_heads, value_heads = group_in
    probs_high, probs_low = sequence_probs(queries, key_heads)
    attended = jnp.einsum('hlm,mhe->lhe', probs_low.astype(jnp.float32), value_heads.astype(jnp.float32))
    return rounded(attended)

def sequence_backward(group_in):
    queries, key_heads, value_heads, grad_attn = group_in
    probs_high, probs_low = sequence_probs(queries, key_heads)
    grad_probs = jnp.einsum('lhe,mhe->hlm', grad_attn.astype(jnp.float32), value_heads.astype(jnp.float32))
    grad_scores = rounded(probs_high * (grad_probs - lax.optimization_barrier(jnp.sum(probs_high * grad_probs, axis=-1, keepdims=True))) / math.sqrt(HEAD_DIM))
    grad_query = rounded(jnp.einsum('hlm,mhe->lhe', grad_scores.astype(jnp.float32), key_heads.astype(jnp.float32)))
    grad_keys = rounded(jnp.einsum('hlm,lhe->mhe', grad_scores.astype(jnp.float32), queries.astype(jnp.float32)))
    grad_values = rounded(jnp.einsum('hlm,lhe->mhe', probs_low.astype(jnp.float32), grad_attn.astype(jnp.float32)))
    return (grad_query, grad_keys, grad_values)

def heads_of(tokens, in_weight, shift_row, scale_row):
    modded, normed, inv_std = normalize(tokens, shift_row, scale_row)
    projected = rounded(jnp.dot(modded.reshape(-1, D), in_weight.reshape(D, 3 * D), preferred_element_type=jnp.float32))
    projected = projected.reshape(tokens.shape[0], tokens.shape[1], 3, HEADS, HEAD_DIM)
    return (projected[:, :, 0], projected[:, :, 1], projected[:, :, 2], normed, inv_std)

def run_forward(queries, key_heads, value_heads, spatial):
    if spatial:
        moved = tuple((jnp.swapaxes(item, 0, 1) for item in (queries, key_heads, value_heads)))
        return jnp.swapaxes(lax.map(sequence_forward, moved), 0, 1)
    return lax.map(sequence_forward, (queries, key_heads, value_heads))

def run_backward(queries, key_heads, value_heads, grad_attn, spatial):
    if spatial:
        moved = tuple((jnp.swapaxes(item, 0, 1) for item in (queries, key_heads, value_heads, grad_attn)))
        outputs = lax.map(sequence_backward, moved)
        return tuple((jnp.swapaxes(item, 0, 1) for item in outputs))
    return lax.map(sequence_backward, (queries, key_heads, value_heads, grad_attn))

def block_forward(tokens, in_weight, out_matrix, shift_row, scale_row, gate_row, spatial):
    queries, key_heads, value_heads, normed, inv_std = heads_of(tokens, in_weight, shift_row, scale_row)
    attended = run_forward(queries, key_heads, value_heads, spatial).reshape(-1, D)
    group_width = D // N_TP
    total = jnp.zeros((attended.shape[0], D), jnp.float32)
    for group in range(N_TP):
        lower = group * group_width
        piece = jnp.dot(attended[:, lower:lower + group_width], out_matrix[lower:lower + group_width, :], preferred_element_type=jnp.float32)
        total = total + rounded(piece).astype(jnp.float32)
    return (tokens.astype(jnp.float32) + gate_row * total.reshape(tokens.shape)).astype(jnp.bfloat16)

def block_backward(tokens, grad, in_weight, out_matrix, shift_row, scale_row, gate_row, spatial):
    queries, key_heads, value_heads, normed, inv_std = heads_of(tokens, in_weight, shift_row, scale_row)
    grad_proj = rounded(gate_row * grad.astype(jnp.float32))
    grad_attn = rounded(jnp.dot(grad_proj.reshape(-1, D), out_matrix.T, preferred_element_type=jnp.float32))
    grad_attn = grad_attn.reshape(queries.shape)
    grad_query, grad_keys, grad_values = run_backward(queries, key_heads, value_heads, grad_attn, spatial)
    stacked = jnp.stack([grad_query, grad_keys, grad_values], axis=2).reshape(-1, 3, D)
    group_width = D // N_TP
    total = jnp.zeros((stacked.shape[0], D), jnp.float32)
    for group in range(N_TP):
        lower = group * group_width
        picked = stacked[:, :, lower:lower + group_width].reshape(-1, 3 * group_width)
        columns = in_weight[:, :, lower:lower + group_width].reshape(D, 3 * group_width)
        piece = jnp.dot(picked, columns.T, preferred_element_type=jnp.float32)
        total = total + rounded(piece).astype(jnp.float32)
    grad_norm = total.reshape(tokens.shape) * (1.0 + scale_row)
    back_part = inv_std * (grad_norm - lax.optimization_barrier(jnp.mean(grad_norm, axis=-1, keepdims=True)) - normed * lax.optimization_barrier(jnp.mean(grad_norm * normed, axis=-1, keepdims=True)))
    return (grad.astype(jnp.float32) + back_part).astype(jnp.bfloat16)

def reference(tokens, grad_out, qkv_weight, out_weight, mod_shift, mod_scale, mod_gate):
    middle = block_forward(tokens, qkv_weight[0], out_weight[0], mod_shift[0], mod_scale[0], mod_gate[0], True)
    result = block_forward(middle, qkv_weight[1], out_weight[1], mod_shift[1], mod_scale[1], mod_gate[1], False)
    grad_mid = block_backward(middle, grad_out, qkv_weight[1], out_weight[1], mod_shift[1], mod_scale[1], mod_gate[1], False)
    grad_in = block_backward(tokens, grad_mid, qkv_weight[0], out_weight[0], mod_shift[0], mod_scale[0], mod_gate[0], True)
    return (result, grad_in)
```

```python
import math

import jax
import jax.numpy as jnp
from jax import lax
from jax.experimental import pallas as pl
from jax.experimental.pallas import tpu as pltpu
from jax.sharding import PartitionSpec as P

D = 1152
HEAD_DIM = 72
HERE = 4
GW = HERE * HEAD_DIM
N_TP = 4
ROWS = 64
INV_ROOT = 1.0 / math.sqrt(HEAD_DIM)
F32 = jnp.float32
BF16 = jnp.bfloat16


def nn(a, b):
    return lax.dot_general(a, b, (((1,), (0,)), ((), ())), preferred_element_type=F32)


def nt(a, b):
    return lax.dot_general(a, b, (((1,), (1,)), ((), ())), preferred_element_type=F32)


def tn(a, b):
    return lax.dot_general(a, b, (((0,), (0,)), ((), ())), preferred_element_type=F32)


def normalize(tokens):
    widened = tokens.astype(F32)
    center = widened - jnp.mean(widened, axis=-1, keepdims=True)
    inv_std = lax.rsqrt(jnp.mean(center * center, axis=-1, keepdims=True) + 1e-06)
    return center * inv_std, inv_std


def norm_back(grad_mod, normed, inv_std, scale_row):
    grad_norm = grad_mod * (1.0 + scale_row)
    return inv_std * (
        grad_norm
        - jnp.mean(grad_norm, axis=-1, keepdims=True)
        - normed * jnp.mean(grad_norm * normed, axis=-1, keepdims=True)
    )


def softmax(scores):
    top = jnp.max(scores, axis=-1, keepdims=True)
    raised = jnp.exp(scores - top)
    return raised / jnp.sum(raised, axis=-1, keepdims=True)


def of_head(array, head):
    lane = lax.broadcasted_iota(jnp.int32, array.shape, 1)
    keep = (lane >= head * HEAD_DIM) & (lane < (head + 1) * HEAD_DIM)
    return jnp.where(keep, array, jnp.zeros_like(array))


def order_matrix(me, rows):
    place = lax.broadcasted_iota(jnp.int32, (rows, 256), 0)
    patch = lax.broadcasted_iota(jnp.int32, (rows, 256), 1)
    wanted = 4 * (place % ROWS) + (me + place // ROWS) % 4
    return (patch == wanted).astype(F32).astype(BF16)


def spatial_forward(me_ref, x_ref, w_ref, ow_ref, shift_ref, scale_ref, p0, p1, p2, p3, qkv_ref, own_ref):
    me = me_ref[0]
    tokens = x_ref[...]
    normed, _ = normalize(tokens)
    modded = (normed * (1.0 + scale_ref[0]) + shift_ref[0]).astype(BF16)
    order = order_matrix(me, 256)
    modded = nn(order, modded).astype(BF16)
    own_ref[...] = nn(order[:ROWS], tokens).astype(BF16)
    queries = nt(modded, w_ref[0, 0]).astype(BF16)
    key_heads = nt(modded, w_ref[0, 1]).astype(BF16)
    value_heads = nt(modded, w_ref[0, 2]).astype(BF16)
    qkv_ref[0] = queries
    qkv_ref[1] = key_heads
    qkv_ref[2] = value_heads
    attended = jnp.zeros((256, GW), F32)
    for head in range(HERE):
        probs = softmax(nt(of_head(queries, head), key_heads) * INV_ROOT)
        attended = attended + nn(probs.astype(BF16), of_head(value_heads, head))
    attended = attended.astype(BF16)
    for k, part in enumerate((p0, p1, p2, p3)):
        part[...] = nn(attended[k * ROWS : (k + 1) * ROWS], ow_ref[0]).astype(BF16)


def temporal(me_ref, m_ref, g_ref, w_ref, ow_ref, shift_ref, scale_ref, gate_ref, *rest):
    part_ref, out_part_ref, kept_ref = rest[-3:]
    mid = m_ref[...]
    kept_ref[0] = mid
    normed, _ = normalize(mid)
    modded = (normed * (1.0 + scale_ref[0]) + shift_ref[0]).astype(BF16)
    queries = nt(modded, w_ref[0, 0]).astype(BF16)
    key_heads = nt(modded, w_ref[0, 1]).astype(BF16)
    value_heads = nt(modded, w_ref[0, 2]).astype(BF16)

    def spread(array):
        return jnp.concatenate([of_head(array, head) for head in range(HERE)], axis=0)

    def gather_heads(array):
        total = of_head(array[:ROWS], 0)
        for head in range(1, HERE):
            total = total + of_head(array[head * ROWS : (head + 1) * ROWS], head)
        return total

    queries_4 = spread(queries)
    probs = softmax(nt(queries_4, key_heads) * INV_ROOT)
    probs_low = probs.astype(BF16)
    grad_proj = (gate_ref[0] * g_ref[0].astype(F32)).astype(BF16)
    grad_attn_4 = spread(nt(grad_proj, ow_ref[0]).astype(BF16))
    grad_probs = nt(grad_attn_4, value_heads)
    grad_scores = (
        probs * (grad_probs - jnp.sum(probs * grad_probs, axis=-1, keepdims=True)) * INV_ROOT
    ).astype(BF16)
    grad_query = gather_heads(nn(grad_scores, key_heads)).astype(BF16)
    grad_keys = tn(grad_scores, queries_4).astype(BF16)
    grad_values = tn(probs_low, grad_attn_4).astype(BF16)
    part = nn(grad_query, w_ref[0, 0]) + nn(grad_keys, w_ref[0, 1]) + nn(grad_values, w_ref[0, 2])
    part_ref[...] = part.astype(BF16)
    attended = gather_heads(nn(probs_low, value_heads)).astype(BF16)
    out_part_ref[0] = nn(attended, ow_ref[0]).astype(BF16)


def spatial_backward(g0, g1, g2, g3, qkv_ref, w_ref, ow_ref, gate_ref, p0, p1, p2, p3):
    grad = jnp.concatenate([g0[...], g1[...], g2[...], g3[...]], axis=0)
    grad_proj = (gate_ref[0] * grad.astype(F32)).astype(BF16)
    grad_attn = nt(grad_proj, ow_ref[0]).astype(BF16)
    queries, key_heads, value_heads = qkv_ref[0], qkv_ref[1], qkv_ref[2]
    grad_query = jnp.zeros((256, GW), F32)
    grad_keys = jnp.zeros((256, GW), F32)
    grad_values = jnp.zeros((256, GW), F32)
    for head in range(HERE):
        query = of_head(queries, head)
        grad_head = of_head(grad_attn, head)
        probs = softmax(nt(query, key_heads) * INV_ROOT)
        grad_probs = nt(grad_head, value_heads)
        grad_scores = (
            probs * (grad_probs - jnp.sum(probs * grad_probs, axis=-1, keepdims=True)) * INV_ROOT
        ).astype(BF16)
        grad_query = grad_query + nn(grad_scores, of_head(key_heads, head))
        grad_keys = grad_keys + tn(grad_scores, query)
        grad_values = grad_values + tn(probs.astype(BF16), grad_head)
    total = (
        nn(grad_query.astype(BF16), w_ref[0, 0])
        + nn(grad_keys.astype(BF16), w_ref[0, 1])
        + nn(grad_values.astype(BF16), w_ref[0, 2])
    )
    for k, part in enumerate((p0, p1, p2, p3)):
        part[...] = total[k * ROWS : (k + 1) * ROWS].astype(BF16)


def mid_of(x_ref, p0, p1, p2, p3, gate_ref, mid_ref):
    total = (p0[...].astype(F32) + p1[...].astype(F32)) + (p2[...].astype(F32) + p3[...].astype(F32))
    mid_ref[...] = (x_ref[...].astype(F32) + gate_ref[0] * total).astype(BF16)


def grad_of(x_ref, g_ref, p0, p1, p2, p3, scale_ref, grad_ref):
    total = (p0[...].astype(F32) + p1[...].astype(F32)) + (p2[...].astype(F32) + p3[...].astype(F32))
    normed, inv_std = normalize(x_ref[...])
    grad = g_ref[...].reshape(ROWS, D).astype(F32)
    grad_ref[...] = (grad + norm_back(total, normed, inv_std, scale_ref[0])).astype(BF16)


def reorder(me_ref, g0, g1, g2, g3, out_ref):
    stacked = jnp.concatenate([g0[...], g1[...], g2[...], g3[...]], axis=0)
    out_ref[...] = tn(order_matrix(me_ref[0], 256), stacked).astype(BF16)


SEMANTICS = pltpu.CompilerParams(vmem_limit_bytes=24 * 1024 * 1024)


def whole(shape):
    return pl.BlockSpec(shape, lambda *_: (0,) * len(shape))


def row_of(block):
    return pl.BlockSpec((1, 1, D), lambda *_: (block, 0, 0))


def rows_out():
    return jax.ShapeDtypeStruct((ROWS, D), BF16)


def run(body, me, operands, specs, out_shape, out_specs, flops, aliases=None):
    return pl.pallas_call(
        body,
        grid_spec=pltpu.PrefetchScalarGridSpec(
            num_scalar_prefetch=0 if me is None else 1,
            grid=(1,),
            in_specs=specs,
            out_specs=out_specs,
        ),
        out_shape=out_shape,
        input_output_aliases=aliases or {},
        compiler_params=SEMANTICS,
        cost_estimate=pl.CostEstimate(flops=flops, bytes_accessed=3_000_000, transcendentals=0),
    )(*(() if me is None else (me,)), *operands)


def shift(array, k):
    return lax.ppermute(array, "tp", [(i, (i + k) % N_TP) for i in range(N_TP)])


def across(array):
    return lax.all_to_all(array, "seq", split_axis=0, concat_axis=0, tiled=True)


def per_device(tokens, grad_out, qkv_weight, out_weight, mod_shift, mod_scale, mod_gate):
    me = lax.axis_index("tp").astype(jnp.int32).reshape(1)
    tokens = tokens.reshape(256, D)
    weights = jnp.transpose(qkv_weight, (0, 2, 3, 1))
    mod_shift, mod_scale, mod_gate = (row.reshape(2, 1, D) for row in (mod_shift, mod_scale, mod_gate))
    quarter = whole((ROWS, D))

    def w_of(block):
        return pl.BlockSpec((1, 3, GW, D), lambda *_: (block, 0, 0, 0))

    def ow_of(block):
        return pl.BlockSpec((1, GW, D), lambda *_: (block, 0, 0))

    p0, p1, p2, p3, qkv_s, own = run(
        spatial_forward,
        me,
        (tokens, weights, out_weight, mod_shift, mod_scale),
        [whole((256, D)), w_of(0), ow_of(0), row_of(0), row_of(0)],
        (rows_out(),) * 4 + (jax.ShapeDtypeStruct((3, 256, GW), BF16), rows_out()),
        (quarter,) * 4 + (whole((3, 256, GW)), quarter),
        1_000_000_000,
    )
    p1, p3, p2 = shift(p1, 1), shift(p3, 3), shift(p2, 2)
    middle = run(
        mid_of, None, (own, p0, p1, p2, p3, mod_gate), [quarter] * 5 + [row_of(0)],
        rows_out(), quarter, 1_000_000,
    )
    mid_own = across(middle)

    mids = [mid_own, shift(mid_own, 1), shift(mid_own, 2), shift(mid_own, 3)]
    parts = [None] * 4
    kept = None
    whole_4 = jax.ShapeDtypeStruct((4, ROWS, D), BF16)
    for k in (0, 1, 3, 2):
        chunk = pl.BlockSpec((1, ROWS, D), lambda _, at, k=k: ((at[0] + 4 - k) % 4, 0, 0))
        anywhere = pl.BlockSpec(memory_space=pl.ANY)
        operands = (mids[k], grad_out, weights, out_weight, mod_shift, mod_scale, mod_gate)
        specs = [quarter, chunk, w_of(1), ow_of(1), row_of(1), row_of(1), row_of(1)]
        aliases = None
        if kept is not None:
            operands, specs, aliases = operands + kept, specs + [anywhere] * 2, {8: 1, 9: 2}
        part, out_part, mid_4 = run(
            temporal, me, operands, specs, (rows_out(), whole_4, whole_4),
            (quarter, chunk, chunk), 500_000_000, aliases,
        )
        kept = (out_part, mid_4)
        parts[k] = shift(part, 4 - k) if k else part
    out_total = lax.psum(kept[0], "tp").astype(F32)
    result = (kept[1].astype(F32) + mod_gate[1] * out_total).astype(BF16)

    own_grad = pl.BlockSpec((1, ROWS, D), lambda _, at: (at[0], 0, 0))
    grad_patch = run(
        lambda me_ref, *refs: grad_of(*refs),
        me, (mid_own, grad_out, *parts, mod_scale), [quarter, own_grad] + [quarter] * 4 + [row_of(1)],
        rows_out(), quarter, 1_000_000,
    )
    grad_own = across(grad_patch)

    grads = [grad_own, shift(grad_own, 3), shift(grad_own, 2), shift(grad_own, 1)]
    b0, b1, b2, b3 = run(
        spatial_backward, None, (*grads, qkv_s, weights, out_weight, mod_gate),
        [quarter] * 4 + [whole((3, 256, GW)), w_of(0), ow_of(0), row_of(0)],
        (rows_out(),) * 4, (quarter,) * 4, 1_500_000_000,
    )
    b1, b3, b2 = shift(b1, 1), shift(b3, 3), shift(b2, 2)
    grad_in_own = run(
        grad_of, None, (own, grad_own, b0, b1, b2, b3, mod_scale), [quarter] * 6 + [row_of(0)],
        rows_out(), quarter, 1_000_000,
    )
    ends = (grad_in_own, shift(grad_in_own, 3), shift(grad_in_own, 2), shift(grad_in_own, 1))
    grad_in = run(
        reorder, me, ends, [quarter] * 4,
        jax.ShapeDtypeStruct((256, D), BF16), whole((256, D)), 100_000_000,
    )
    return (result, grad_in.reshape(256, 1, D))


def solution(mesh):
    in_specs = (
        P(None, "seq", None),
        P("seq", None, None),
        P(None, None, None, "tp"),
        P(None, "tp", None),
        P(),
        P(),
        P(),
    )
    out_specs = (P("seq", None, None), P(None, "seq", None))
    return jax.shard_map(
        per_device, mesh=mesh, in_specs=in_specs, out_specs=out_specs, check_vma=False
    )
```

```python
import math

import jax
import jax.numpy as jnp
from jax import lax
from jax.experimental import pallas as pl
from jax.experimental.pallas import tpu as pltpu
from jax.sharding import PartitionSpec as P

D = 1152
HEAD_DIM = 72
HERE = 4
GW = HERE * HEAD_DIM
N_TP = 4
ROWS = 64
HALF = 32
INV_ROOT = 1.0 / math.sqrt(HEAD_DIM)
F32 = jnp.float32
BF16 = jnp.bfloat16


def nn(a, b):
    return lax.dot_general(a, b, (((1,), (0,)), ((), ())), preferred_element_type=F32)


def nt(a, b):
    return lax.dot_general(a, b, (((1,), (1,)), ((), ())), preferred_element_type=F32)


def tn(a, b):
    return lax.dot_general(a, b, (((0,), (0,)), ((), ())), preferred_element_type=F32)


def normalize(tokens):
    widened = tokens.astype(F32)
    center = widened - jnp.mean(widened, axis=-1, keepdims=True)
    inv_std = lax.rsqrt(jnp.mean(center * center, axis=-1, keepdims=True) + 1e-06)
    return center * inv_std, inv_std


def norm_back(grad_mod, normed, inv_std, scale_row):
    grad_norm = grad_mod * (1.0 + scale_row)
    return inv_std * (
        grad_norm
        - jnp.mean(grad_norm, axis=-1, keepdims=True)
        - normed * jnp.mean(grad_norm * normed, axis=-1, keepdims=True)
    )


def softmax(scores):
    top = jnp.max(scores, axis=-1, keepdims=True)
    raised = jnp.exp(scores - top)
    return raised / jnp.sum(raised, axis=-1, keepdims=True)


def of_head(array, head):
    lane = lax.broadcasted_iota(jnp.int32, array.shape, 1)
    keep = (lane >= head * HEAD_DIM) & (lane < (head + 1) * HEAD_DIM)
    return jnp.where(keep, array, jnp.zeros_like(array))


def order_matrix(first, rows):
    place = lax.broadcasted_iota(jnp.int32, (rows, 256), 0)
    patch = lax.broadcasted_iota(jnp.int32, (rows, 256), 1)
    return (patch == 4 * (place % ROWS) + first + place // ROWS).astype(F32).astype(BF16)


def chunk_rows(chunk):
    return pl.ds(pl.multiple_of(chunk * ROWS, ROWS), ROWS)


def fetch(sources, buffers, sems):
    copies = [
        pltpu.make_async_copy(source, buffer, sems.at[i])
        for i, (source, buffer) in enumerate(zip(sources, buffers))
    ]
    for copy in copies:
        copy.start()
    return copies


def project(modded, weights):
    joined = nt(modded, weights)
    return tuple(joined[:, i * GW : (i + 1) * GW].astype(BF16) for i in range(3))


def spatial_forward(
    me_ref, x_hbm, w_hbm, ow_hbm, shift_ref, scale_ref,
    p0, p1, p2, p3, qkv_ref, own_ref, x_ref, w_ref, ow_ref, attended_ref, sems,
):
    x_copy, w_copy, ow_copy = fetch(
        (x_hbm, w_hbm.at[0], ow_hbm.at[0]), (x_ref, w_ref, ow_ref), sems
    )
    me = me_ref[0]
    x_copy.wait()
    tokens = x_ref[...]
    normed, _ = normalize(tokens)
    modded = (normed * (1.0 + scale_ref[0:1]) + shift_ref[0:1]).astype(BF16)
    modded = nn(order_matrix(0, 256), modded).astype(BF16)
    own_ref[...] = nn(order_matrix(me, ROWS), tokens).astype(BF16)
    w_copy.wait()
    queries, key_heads, value_heads = project(modded, w_ref[...])
    qkv_ref[0] = queries
    qkv_ref[1] = key_heads
    qkv_ref[2] = value_heads
    attended = jnp.zeros((256, GW), F32)
    for head in range(HERE):
        probs = softmax(nt(of_head(queries, head), key_heads) * INV_ROOT)
        attended = attended + nn(probs.astype(BF16), of_head(value_heads, head))
    ow_copy.wait()
    attended_ref[...] = nn(attended.astype(BF16), ow_ref[...]).astype(BF16)
    for k, part in enumerate((p0, p1, p2, p3)):
        part[...] = attended_ref[chunk_rows((me + k) % 4), :]


def temporal(me_ref, m_ref, g_ref, w_ref, ow_ref, shift_ref, scale_ref, gate_ref, both_ref):
    part_ref, out_part_ref = both_ref.at[:ROWS], both_ref.at[ROWS:]
    mid = m_ref[...]
    normed, _ = normalize(mid)
    modded = (normed * (1.0 + scale_ref[1:2]) + shift_ref[1:2]).astype(BF16)
    grad_proj = (gate_ref[1:2] * g_ref[...].astype(F32)).astype(BF16)
    queries, key_heads, value_heads = project(modded, w_ref[...])

    def spread(array):
        return jnp.concatenate([of_head(array, head) for head in range(HERE)], axis=0)

    def gather_heads(array):
        total = of_head(array[:ROWS], 0)
        for head in range(1, HERE):
            total = total + of_head(array[head * ROWS : (head + 1) * ROWS], head)
        return total

    queries_4 = spread(queries)
    probs = softmax(nt(queries_4, key_heads) * INV_ROOT)
    probs_low = probs.astype(BF16)
    grad_attn_4 = spread(nt(grad_proj, ow_ref[...]).astype(BF16))
    grad_probs = nt(grad_attn_4, value_heads)
    grad_scores = (
        probs * (grad_probs - jnp.sum(probs * grad_probs, axis=-1, keepdims=True)) * INV_ROOT
    ).astype(BF16)
    grad_query = gather_heads(nn(grad_scores, key_heads))
    grad_keys = tn(grad_scores, queries_4)
    grad_values = tn(probs_low, grad_attn_4)
    joined = jnp.concatenate([grad_query, grad_keys, grad_values], axis=1).astype(BF16)
    part_ref[...] = nn(joined, w_ref[...]).astype(BF16)
    attended = gather_heads(nn(probs_low, value_heads)).astype(BF16)
    out_part_ref[...] = nn(attended, ow_ref[...]).astype(BF16)


def spatial_backward(
    me_ref, grad_ref, qkv_ref, w_ref, ow_ref, gate_ref, p0, p1, p2, p3, total_ref
):
    grad = jnp.concatenate([grad_ref[chunk] for chunk in range(4)], axis=0)
    grad_proj = (gate_ref[0:1] * grad.astype(F32)).astype(BF16)
    grad_attn = nt(grad_proj, ow_ref[...]).astype(BF16)
    queries, key_heads, value_heads = qkv_ref[0], qkv_ref[1], qkv_ref[2]
    grad_query = jnp.zeros((256, GW), F32)
    grad_keys = jnp.zeros((256, GW), F32)
    grad_values = jnp.zeros((256, GW), F32)
    for head in range(HERE):
        query = of_head(queries, head)
        grad_head = of_head(grad_attn, head)
        probs = softmax(nt(query, key_heads) * INV_ROOT)
        grad_probs = nt(grad_head, value_heads)
        grad_scores = (
            probs * (grad_probs - jnp.sum(probs * grad_probs, axis=-1, keepdims=True)) * INV_ROOT
        ).astype(BF16)
        grad_query = grad_query + nn(grad_scores, of_head(key_heads, head))
        grad_keys = grad_keys + tn(grad_scores, query)
        grad_values = grad_values + tn(probs.astype(BF16), grad_head)
    joined = jnp.concatenate([grad_query, grad_keys, grad_values], axis=1).astype(BF16)
    total_ref[...] = nn(joined, w_ref[...]).astype(BF16)
    for k, part in enumerate((p0, p1, p2, p3)):
        part[...] = total_ref[chunk_rows((me_ref[0] + k) % 4), :]


def add_in(a_ref, b_ref, sum_ref):
    sum_ref[...] = a_ref[...].astype(F32) + b_ref[...].astype(F32)


def block_out(block, x_ref, gate_ref, *refs):
    total = refs[0][...].astype(F32)
    for ref in refs[1:-1]:
        total = total + ref[...].astype(F32)
    refs[-1][...] = (x_ref[...].astype(F32) + gate_ref[block : block + 1] * total).astype(BF16)


def grad_of(block, x_ref, g_ref, scale_ref, *refs):
    total = refs[0][...].astype(F32)
    for ref in refs[1:-1]:
        total = total + ref[...].astype(F32)
    normed, inv_std = normalize(x_ref[...])
    grad = g_ref[...].astype(F32)
    back = norm_back(total, normed, inv_std, scale_ref[block : block + 1])
    refs[-1][...] = (grad + back).astype(BF16)


def pack(grad_ref, x_ref, gate_ref, *refs):
    sent_ref, later_ref = refs[-2:]
    total = refs[0][...].astype(F32)
    for ref in refs[1:-2]:
        total = total + ref[...].astype(F32)
    result = (x_ref[...].astype(F32) + gate_ref[1:2] * total).astype(BF16)
    sent_ref[:ROWS] = grad_ref[...]
    sent_ref[ROWS:] = result[:HALF]
    later_ref[...] = result[HALF:]


def pack_last(x_ref, g_ref, scale_ref, b0, b1, b2, b3, later_ref, sent_ref):
    grad_of(0, x_ref, g_ref, scale_ref, b0, b1, b2, b3, sent_ref.at[:ROWS])
    sent_ref[ROWS:] = later_ref[...]


def unpack(first_ref, last_ref, ends_ref, result_ref, grad_ref):
    stacked = jnp.concatenate([ends_ref[chunk] for chunk in range(4)], axis=0)
    grad_ref[...] = tn(order_matrix(0, 256), stacked).astype(BF16)
    result_ref[:, :HALF] = first_ref[...]
    result_ref[:, HALF:] = last_ref[...]


IN_HBM = pl.BlockSpec(memory_space=pltpu.HBM)


def whole(shape):
    return pl.BlockSpec(shape, lambda *_: (0,) * len(shape))


QUARTER = whole((ROWS, D))
VECTORS = whole((2, D))


def rows_out(dtype=BF16):
    return jax.ShapeDtypeStruct((ROWS, D), dtype)


def run(
    body, me, operands, specs, out_shape, out_specs, flops,
    aliases=None, scratch=(), mib=24, moved=0,
):
    return pl.pallas_call(
        body,
        grid_spec=pltpu.PrefetchScalarGridSpec(
            num_scalar_prefetch=0 if me is None else 1,
            grid=(1,),
            in_specs=specs,
            out_specs=out_specs,
            scratch_shapes=list(scratch),
        ),
        out_shape=out_shape,
        input_output_aliases=aliases or {},
        compiler_params=pltpu.CompilerParams(vmem_limit_bytes=mib * 1024 * 1024),
        cost_estimate=pl.CostEstimate(flops=flops, bytes_accessed=moved, transcendentals=0),
    )(*(() if me is None else (me,)), *operands)


def shift(array, k):
    return lax.ppermute(array, "tp", [(i, (i + k) % N_TP) for i in range(N_TP)])


def across(array):
    return lax.all_to_all(array, "seq", split_axis=0, concat_axis=0, tiled=True)


def weights_of(block, weights, out_weight, after):
    weights, out_weight, _ = lax.optimization_barrier((weights, out_weight, after))
    return weights[block], out_weight[block]


def per_device(tokens, grad_out, qkv_weight, out_weight, mod_shift, mod_scale, mod_gate):
    me = lax.axis_index("tp").astype(jnp.int32).reshape(1)
    tokens = tokens.reshape(256, D)
    weights = jnp.transpose(qkv_weight, (0, 2, 3, 1)).reshape(2, 3 * GW, D)
    qkv_spec = whole((3, 256, GW))

    p0, p1, p2, p3, qkv_s, own = run(
        spatial_forward,
        me,
        (tokens, weights, out_weight, mod_shift, mod_scale),
        [IN_HBM, IN_HBM, IN_HBM, VECTORS, VECTORS],
        (rows_out(),) * 4 + (jax.ShapeDtypeStruct((3, 256, GW), BF16), rows_out()),
        (QUARTER,) * 4 + (qkv_spec, QUARTER),
        1_000_000_000,
        scratch=(
            pltpu.VMEM((256, D), BF16),
            pltpu.VMEM((3 * GW, D), BF16),
            pltpu.VMEM((GW, D), BF16),
            pltpu.VMEM((256, D), BF16),
            pltpu.SemaphoreType.DMA((3,)),
        ),
        mib=58,
    )
    p1, p3, p2 = shift(p1, 1), shift(p3, 3), shift(p2, 2)
    early = run(add_in, None, (p0, p1), [QUARTER] * 2, rows_out(F32), QUARTER, 350_000_000)
    middle = run(
        lambda *refs: block_out(0, *refs),
        None, (own, mod_gate, early, p3, p2), [QUARTER, VECTORS] + [QUARTER] * 3,
        rows_out(), QUARTER, 1_000_000,
    )
    mid_own = across(middle)
    w_spec, ow_spec = whole((3 * GW, D)), whole((GW, D))
    w1, ow1 = weights_of(1, weights, out_weight, mid_own)

    mids = lax.all_gather(mid_own, "tp")
    both = jax.ShapeDtypeStruct((2 * ROWS, D), BF16)
    sent = {}
    for k in (2, 1, 3, 0):
        chunk = pl.BlockSpec((None, ROWS, D), lambda _, at, k=k: ((at[0] + 4 - k) % 4, 0, 0))
        sent[k] = run(
            temporal, me, (mids, grad_out, w1, ow1, mod_shift, mod_scale, mod_gate),
            [chunk, chunk, w_spec, ow_spec, VECTORS, VECTORS, VECTORS],
            both, whole((2 * ROWS, D)), 50_000_000 if k else 350_000_000,
        )
        if k:
            sent[k] = shift(sent[k], 4 - k)
    later = pl.BlockSpec((ROWS, D), lambda *_: (1, 0))
    total = sent[0]
    for k in (2, 1):
        total = run(
            add_in, None, (total, sent[k]), [QUARTER] * 2, rows_out(F32), QUARTER, 350_000_000
        )

    own_grad = pl.BlockSpec((None, ROWS, D), lambda _, at: (at[0], 0, 0))
    grad_patch = run(
        lambda me_ref, *refs: grad_of(1, *refs),
        me, (mid_own, grad_out, mod_scale, total, sent[3]),
        [QUARTER, own_grad, VECTORS] + [QUARTER] * 2,
        rows_out(), QUARTER, 1_000_000,
    )
    grad_own = across(grad_patch)
    w0, ow0 = weights_of(0, weights, out_weight, grad_own)
    message = jax.ShapeDtypeStruct((ROWS + HALF, D), BF16)
    half = whole((HALF, D))
    packed, result_later = run(
        pack, None, (grad_own, mid_own, mod_gate, *(sent[k] for k in range(4))),
        [QUARTER, QUARTER, VECTORS] + [later] * 4,
        (message, jax.ShapeDtypeStruct((HALF, D), BF16)),
        (whole((ROWS + HALF, D)), half), 1_000_000,
    )
    grads = lax.all_gather(packed, "tp")
    front, back = whole((4, ROWS, D)), pl.BlockSpec((4, HALF, D), lambda *_: (0, 2, 0))
    b0, b1, b2, b3 = run(
        spatial_backward, me, (grads, qkv_s, w0, ow0, mod_gate),
        [front, qkv_spec, w_spec, ow_spec, VECTORS],
        (rows_out(),) * 4, (QUARTER,) * 4, 1_500_000_000,
        scratch=(pltpu.VMEM((256, D), BF16),),
    )
    b1, b3, b2 = shift(b1, 1), shift(b3, 3), shift(b2, 2)
    packed = run(
        pack_last, None, (own, grad_own, mod_scale, b0, b1, b2, b3, result_later),
        [QUARTER] * 2 + [VECTORS] + [QUARTER] * 4 + [half],
        message, whole((ROWS + HALF, D)), 1_000_000,
    )
    ends = lax.all_gather(packed, "tp")
    result, grad_in = run(
        unpack, None, (grads, ends, ends), [back, back, front],
        (jax.ShapeDtypeStruct((4, ROWS, D), BF16), jax.ShapeDtypeStruct((256, D), BF16)),
        (whole((4, ROWS, D)), whole((256, D))), 100_000_000,
    )
    return (result, grad_in.reshape(256, 1, D))


def solution(mesh):
    in_specs = (
        P(None, "seq", None),
        P("seq", None, None),
        P(None, None, None, "tp"),
        P(None, "tp", None),
        P(),
        P(),
        P(),
    )
    out_specs = (P("seq", None, None), P(None, "seq", None))
    return jax.shard_map(
        per_device, mesh=mesh, in_specs=in_specs, out_specs=out_specs, check_vma=False
    )
```

```python
import math

import jax
import jax.numpy as jnp
from jax import lax
from jax.experimental import pallas as pl
from jax.experimental.pallas import tpu as pltpu
from jax.sharding import PartitionSpec as P

D = 1152
HEAD_DIM = 72
HERE = 4
GW = HERE * HEAD_DIM
N_TP = 4
ROWS = 64
HALF = 32
RESULT_FLOPS = 3_000_000_000
INV_ROOT = 1.0 / math.sqrt(HEAD_DIM)
F32 = jnp.float32
BF16 = jnp.bfloat16


def nn(a, b):
    return lax.dot_general(a, b, (((1,), (0,)), ((), ())), preferred_element_type=F32)


def nt(a, b):
    return lax.dot_general(a, b, (((1,), (1,)), ((), ())), preferred_element_type=F32)


def tn(a, b):
    return lax.dot_general(a, b, (((0,), (0,)), ((), ())), preferred_element_type=F32)


def normalize(tokens):
    widened = tokens.astype(F32)
    center = widened - jnp.mean(widened, axis=-1, keepdims=True)
    inv_std = lax.rsqrt(jnp.mean(center * center, axis=-1, keepdims=True) + 1e-06)
    return center * inv_std, inv_std


def norm_back(grad_mod, normed, inv_std, scale_row):
    grad_norm = grad_mod * (1.0 + scale_row)
    return inv_std * (
        grad_norm
        - jnp.mean(grad_norm, axis=-1, keepdims=True)
        - normed * jnp.mean(grad_norm * normed, axis=-1, keepdims=True)
    )


def softmax(scores):
    top = jnp.max(scores, axis=-1, keepdims=True)
    raised = jnp.exp(scores - top)
    return raised / jnp.sum(raised, axis=-1, keepdims=True)


def of_head(array, head):
    lane = lax.broadcasted_iota(jnp.int32, array.shape, 1)
    keep = (lane >= head * HEAD_DIM) & (lane < (head + 1) * HEAD_DIM)
    return jnp.where(keep, array, jnp.zeros_like(array))


def order_matrix(first, rows):
    place = lax.broadcasted_iota(jnp.int32, (rows, 256), 0)
    patch = lax.broadcasted_iota(jnp.int32, (rows, 256), 1)
    return (patch == 4 * (place % ROWS) + first + place // ROWS).astype(F32).astype(BF16)


def chunk_rows(chunk):
    return pl.ds(pl.multiple_of(chunk * ROWS, ROWS), ROWS)


def fetch(sources, buffers, sems):
    copies = [
        pltpu.make_async_copy(source, buffer, sems.at[i])
        for i, (source, buffer) in enumerate(zip(sources, buffers))
    ]
    for copy in copies:
        copy.start()
    return copies


def project(modded, weights):
    joined = nt(modded, weights)
    return tuple(joined[:, i * GW : (i + 1) * GW].astype(BF16) for i in range(3))


def spatial_forward(
    me_ref, x_hbm, w_hbm, ow_hbm, shift_ref, scale_ref,
    p0, p1, p2, p3, qkv_ref, own_ref, x_ref, w_ref, ow_ref, attended_ref, sems,
):
    x_copy, w_copy, ow_copy = fetch(
        (x_hbm, w_hbm.at[0], ow_hbm.at[0]), (x_ref, w_ref, ow_ref), sems
    )
    me = me_ref[0]
    x_copy.wait()
    tokens = x_ref[...]
    normed, _ = normalize(tokens)
    modded = (normed * (1.0 + scale_ref[0:1]) + shift_ref[0:1]).astype(BF16)
    modded = nn(order_matrix(0, 256), modded).astype(BF16)
    own_ref[...] = nn(order_matrix(me, ROWS), tokens).astype(BF16)
    w_copy.wait()
    queries, key_heads, value_heads = project(modded, w_ref[...])
    qkv_ref[0] = queries
    qkv_ref[1] = key_heads
    qkv_ref[2] = value_heads
    attended = jnp.zeros((256, GW), F32)
    for head in range(HERE):
        probs = softmax(nt(of_head(queries, head), key_heads) * INV_ROOT)
        attended = attended + nn(probs.astype(BF16), of_head(value_heads, head))
    ow_copy.wait()
    attended_ref[...] = nn(attended.astype(BF16), ow_ref[...]).astype(BF16)
    for k, part in enumerate((p0, p1, p2, p3)):
        part[...] = attended_ref[chunk_rows((me + k) % 4), :]


def temporal(me_ref, m_ref, g_ref, w_ref, ow_ref, shift_ref, scale_ref, gate_ref, part_ref, out_part_ref):
    mid = m_ref[...]
    normed, _ = normalize(mid)
    modded = (normed * (1.0 + scale_ref[1:2]) + shift_ref[1:2]).astype(BF16)
    grad_proj = (gate_ref[1:2] * g_ref[...].astype(F32)).astype(BF16)
    queries, key_heads, value_heads = project(modded, w_ref[...])

    def spread(array):
        return jnp.concatenate([of_head(array, head) for head in range(HERE)], axis=0)

    def gather_heads(array):
        total = of_head(array[:ROWS], 0)
        for head in range(1, HERE):
            total = total + of_head(array[head * ROWS : (head + 1) * ROWS], head)
        return total

    queries_4 = spread(queries)
    probs = softmax(nt(queries_4, key_heads) * INV_ROOT)
    probs_low = probs.astype(BF16)
    grad_attn_4 = spread(nt(grad_proj, ow_ref[...]).astype(BF16))
    grad_probs = nt(grad_attn_4, value_heads)
    grad_scores = (
        probs * (grad_probs - jnp.sum(probs * grad_probs, axis=-1, keepdims=True)) * INV_ROOT
    ).astype(BF16)
    grad_query = gather_heads(nn(grad_scores, key_heads))
    grad_keys = tn(grad_scores, queries_4)
    grad_values = tn(probs_low, grad_attn_4)
    joined = jnp.concatenate([grad_query, grad_keys, grad_values], axis=1).astype(BF16)
    part_ref[...] = nn(joined, w_ref[...]).astype(BF16)
    attended = gather_heads(nn(probs_low, value_heads)).astype(BF16)
    out_part_ref[...] = nn(attended, ow_ref[...]).astype(BF16)


def spatial_backward(
    me_ref, grad_ref, qkv_ref, w_ref, ow_ref, gate_ref, p0, p1, p2, p3, total_ref
):
    grad = jnp.concatenate([grad_ref[chunk] for chunk in range(4)], axis=0)
    grad_proj = (gate_ref[0:1] * grad.astype(F32)).astype(BF16)
    grad_attn = nt(grad_proj, ow_ref[...]).astype(BF16)
    queries, key_heads, value_heads = qkv_ref[0], qkv_ref[1], qkv_ref[2]
    grad_query = jnp.zeros((256, GW), F32)
    grad_keys = jnp.zeros((256, GW), F32)
    grad_values = jnp.zeros((256, GW), F32)
    for head in range(HERE):
        query = of_head(queries, head)
        grad_head = of_head(grad_attn, head)
        probs = softmax(nt(query, key_heads) * INV_ROOT)
        grad_probs = nt(grad_head, value_heads)
        grad_scores = (
            probs * (grad_probs - jnp.sum(probs * grad_probs, axis=-1, keepdims=True)) * INV_ROOT
        ).astype(BF16)
        grad_query = grad_query + nn(grad_scores, of_head(key_heads, head))
        grad_keys = grad_keys + tn(grad_scores, query)
        grad_values = grad_values + tn(probs.astype(BF16), grad_head)
    joined = jnp.concatenate([grad_query, grad_keys, grad_values], axis=1).astype(BF16)
    total_ref[...] = nn(joined, w_ref[...]).astype(BF16)
    for k, part in enumerate((p0, p1, p2, p3)):
        part[...] = total_ref[chunk_rows((me_ref[0] + k) % 4), :]


def add_in(a_ref, b_ref, sum_ref):
    sum_ref[...] = a_ref[...].astype(F32) + b_ref[...].astype(F32)


def block_out(block, x_ref, gate_ref, *refs):
    total = refs[0][...].astype(F32)
    for ref in refs[1:-1]:
        total = total + ref[...].astype(F32)
    refs[-1][...] = (x_ref[...].astype(F32) + gate_ref[block : block + 1] * total).astype(BF16)


def grad_of(block, x_ref, g_ref, scale_ref, *refs):
    total = refs[0][...].astype(F32)
    for ref in refs[1:-1]:
        total = total + ref[...].astype(F32)
    normed, inv_std = normalize(x_ref[...])
    grad = g_ref[...].astype(F32)
    back = norm_back(total, normed, inv_std, scale_ref[block : block + 1])
    refs[-1][...] = (grad + back).astype(BF16)


def pack(grad_ref, result_ref, sent_ref):
    sent_ref[:ROWS] = grad_ref[...]
    sent_ref[ROWS:] = result_ref[:HALF]


def pack_last(x_ref, g_ref, scale_ref, b0, b1, b2, b3, result_ref, sent_ref):
    grad_of(0, x_ref, g_ref, scale_ref, b0, b1, b2, b3, sent_ref.at[:ROWS])
    sent_ref[ROWS:] = result_ref[HALF:]


def unpack(first_ref, last_ref, ends_ref, result_ref, grad_ref):
    stacked = jnp.concatenate([ends_ref[chunk] for chunk in range(4)], axis=0)
    grad_ref[...] = tn(order_matrix(0, 256), stacked).astype(BF16)
    result_ref[:, :HALF] = first_ref[...]
    result_ref[:, HALF:] = last_ref[...]


IN_HBM = pl.BlockSpec(memory_space=pltpu.HBM)


def whole(shape):
    return pl.BlockSpec(shape, lambda *_: (0,) * len(shape))


QUARTER = whole((ROWS, D))
VECTORS = whole((2, D))


def rows_out(dtype=BF16):
    return jax.ShapeDtypeStruct((ROWS, D), dtype)


def run(
    body, me, operands, specs, out_shape, out_specs, flops,
    aliases=None, scratch=(), mib=24, moved=0,
):
    return pl.pallas_call(
        body,
        grid_spec=pltpu.PrefetchScalarGridSpec(
            num_scalar_prefetch=0 if me is None else 1,
            grid=(1,),
            in_specs=specs,
            out_specs=out_specs,
            scratch_shapes=list(scratch),
        ),
        out_shape=out_shape,
        input_output_aliases=aliases or {},
        compiler_params=pltpu.CompilerParams(vmem_limit_bytes=mib * 1024 * 1024),
        cost_estimate=pl.CostEstimate(flops=flops, bytes_accessed=moved, transcendentals=0),
    )(*(() if me is None else (me,)), *operands)


def shift(array, k):
    return lax.ppermute(array, "tp", [(i, (i + k) % N_TP) for i in range(N_TP)])


def across(array):
    return lax.all_to_all(array, "seq", split_axis=0, concat_axis=0, tiled=True)


def weights_of(block, weights, out_weight, after):
    weights, out_weight, _ = lax.optimization_barrier((weights, out_weight, after))
    return weights[block], out_weight[block]


def per_device(tokens, grad_out, qkv_weight, out_weight, mod_shift, mod_scale, mod_gate):
    me = lax.axis_index("tp").astype(jnp.int32).reshape(1)
    tokens = tokens.reshape(256, D)
    weights = jnp.transpose(qkv_weight, (0, 2, 3, 1)).reshape(2, 3 * GW, D)
    qkv_spec = whole((3, 256, GW))

    p0, p1, p2, p3, qkv_s, own = run(
        spatial_forward,
        me,
        (tokens, weights, out_weight, mod_shift, mod_scale),
        [IN_HBM, IN_HBM, IN_HBM, VECTORS, VECTORS],
        (rows_out(),) * 4 + (jax.ShapeDtypeStruct((3, 256, GW), BF16), rows_out()),
        (QUARTER,) * 4 + (qkv_spec, QUARTER),
        1_000_000_000,
        scratch=(
            pltpu.VMEM((256, D), BF16),
            pltpu.VMEM((3 * GW, D), BF16),
            pltpu.VMEM((GW, D), BF16),
            pltpu.VMEM((256, D), BF16),
            pltpu.SemaphoreType.DMA((3,)),
        ),
        mib=58,
    )
    p1, p3, p2 = shift(p1, 1), shift(p3, 3), shift(p2, 2)
    early = run(add_in, None, (p0, p1), [QUARTER] * 2, rows_out(F32), QUARTER, 350_000_000)
    middle = run(
        lambda *refs: block_out(0, *refs),
        None, (own, mod_gate, early, p3, p2), [QUARTER, VECTORS] + [QUARTER] * 3,
        rows_out(), QUARTER, 1_000_000,
    )
    mid_own = across(middle)
    w_spec, ow_spec = whole((3 * GW, D)), whole((GW, D))
    w1, ow1 = weights_of(1, weights, out_weight, mid_own)

    mids = lax.all_gather(mid_own, "tp")
    sent, outs = {}, {}
    for k in (2, 1, 3, 0):
        chunk = pl.BlockSpec((None, ROWS, D), lambda _, at, k=k: ((at[0] + 4 - k) % 4, 0, 0))
        sent[k], outs[k] = run(
            temporal, me, (mids, grad_out, w1, ow1, mod_shift, mod_scale, mod_gate),
            [chunk, chunk, w_spec, ow_spec, VECTORS, VECTORS, VECTORS],
            (rows_out(), rows_out()), (QUARTER, QUARTER), 50_000_000 if k else 350_000_000,
        )
        if k:
            sent[k] = shift(sent[k], 4 - k)
    total = sent[0]
    for k in (2, 1):
        total = run(
            add_in, None, (total, sent[k]), [QUARTER] * 2, rows_out(F32), QUARTER, 350_000_000
        )
    outs = dict(zip(outs, lax.optimization_barrier(tuple(outs.values()))))
    for k in (2, 1, 3):
        outs[k] = shift(outs[k], 4 - k)
    result_own = run(
        lambda *refs: block_out(1, *refs),
        None, (mid_own, mod_gate, *(outs[k] for k in range(4))),
        [QUARTER, VECTORS] + [QUARTER] * 4, rows_out(), QUARTER, RESULT_FLOPS,
    )

    own_grad = pl.BlockSpec((None, ROWS, D), lambda _, at: (at[0], 0, 0))
    grad_patch = run(
        lambda me_ref, *refs: grad_of(1, *refs),
        me, (mid_own, grad_out, mod_scale, total, sent[3]),
        [QUARTER, own_grad, VECTORS] + [QUARTER] * 2,
        rows_out(), QUARTER, 1_000_000,
    )
    grad_own = across(grad_patch)
    w0, ow0 = weights_of(0, weights, out_weight, grad_own)
    message = jax.ShapeDtypeStruct((ROWS + HALF, D), BF16)
    packed = run(
        pack, None, (grad_own, result_own), [QUARTER, QUARTER],
        message, whole((ROWS + HALF, D)), 1_000_000,
    )
    grads = lax.all_gather(packed, "tp")
    front, back = whole((4, ROWS, D)), pl.BlockSpec((4, HALF, D), lambda *_: (0, 2, 0))
    b0, b1, b2, b3 = run(
        spatial_backward, me, (grads, qkv_s, w0, ow0, mod_gate),
        [front, qkv_spec, w_spec, ow_spec, VECTORS],
        (rows_out(),) * 4, (QUARTER,) * 4, 1_500_000_000,
        scratch=(pltpu.VMEM((256, D), BF16),),
    )
    b1, b3, b2 = shift(b1, 1), shift(b3, 3), shift(b2, 2)
    packed = run(
        pack_last, None, (own, grad_own, mod_scale, b0, b1, b2, b3, result_own),
        [QUARTER] * 2 + [VECTORS] + [QUARTER] * 5,
        message, whole((ROWS + HALF, D)), 1_000_000,
    )
    ends = lax.all_gather(packed, "tp")
    result, grad_in = run(
        unpack, None, (grads, ends, ends), [back, back, front],
        (jax.ShapeDtypeStruct((4, ROWS, D), BF16), jax.ShapeDtypeStruct((256, D), BF16)),
        (whole((4, ROWS, D)), whole((256, D))), 100_000_000,
    )
    return (result, grad_in.reshape(256, 1, D))


def solution(mesh):
    in_specs = (
        P(None, "seq", None),
        P("seq", None, None),
        P(None, None, None, "tp"),
        P(None, "tp", None),
        P(),
        P(),
        P(),
    )
    out_specs = (P("seq", None, None), P(None, "seq", None))
    return jax.shard_map(
        per_device, mesh=mesh, in_specs=in_specs, out_specs=out_specs, check_vma=False
    )
```

```python
import math

import jax
import jax.numpy as jnp
from jax import lax
from jax.experimental import pallas as pl
from jax.experimental.pallas import tpu as pltpu
from jax.sharding import PartitionSpec as P

D = 1152
HEAD_DIM = 72
HERE = 4
GW = HERE * HEAD_DIM
N_TP = 4
ROWS = 64
HALF = 32
RESULT_FLOPS = 3_000_000_000
INV_ROOT = 1.0 / math.sqrt(HEAD_DIM)
F32 = jnp.float32
BF16 = jnp.bfloat16


def nn(a, b):
    return lax.dot_general(a, b, (((1,), (0,)), ((), ())), preferred_element_type=F32)


def nt(a, b):
    return lax.dot_general(a, b, (((1,), (1,)), ((), ())), preferred_element_type=F32)


def tn(a, b):
    return lax.dot_general(a, b, (((0,), (0,)), ((), ())), preferred_element_type=F32)


def normalize(tokens):
    widened = tokens.astype(F32)
    center = widened - jnp.mean(widened, axis=-1, keepdims=True)
    inv_std = lax.rsqrt(jnp.mean(center * center, axis=-1, keepdims=True) + 1e-06)
    return center * inv_std, inv_std


def norm_back(grad_mod, normed, inv_std, scale_row):
    grad_norm = grad_mod * (1.0 + scale_row)
    return inv_std * (
        grad_norm
        - jnp.mean(grad_norm, axis=-1, keepdims=True)
        - normed * jnp.mean(grad_norm * normed, axis=-1, keepdims=True)
    )


def softmax(scores):
    top = jnp.max(scores, axis=-1, keepdims=True)
    raised = jnp.exp(scores - top)
    return raised / jnp.sum(raised, axis=-1, keepdims=True)


def of_head(array, head):
    lane = lax.broadcasted_iota(jnp.int32, array.shape, 1)
    keep = (lane >= head * HEAD_DIM) & (lane < (head + 1) * HEAD_DIM)
    return jnp.where(keep, array, jnp.zeros_like(array))


def pairs(array):
    return array[:, : GW // 2], array[:, GW // 2 :]


def order_matrix(first, rows):
    place = lax.broadcasted_iota(jnp.int32, (rows, 256), 0)
    patch = lax.broadcasted_iota(jnp.int32, (rows, 256), 1)
    return (patch == 4 * (place % ROWS) + first + place // ROWS).astype(F32).astype(BF16)


def chunk_rows(chunk):
    return pl.ds(pl.multiple_of(chunk * ROWS, ROWS), ROWS)


def fetch(sources, buffers, sems):
    copies = [
        pltpu.make_async_copy(source, buffer, sems.at[i])
        for i, (source, buffer) in enumerate(zip(sources, buffers))
    ]
    for copy in copies:
        copy.start()
    return copies


def project(modded, weights):
    joined = nt(modded, weights)
    return tuple(joined[:, i * GW : (i + 1) * GW].astype(BF16) for i in range(3))


def spatial_forward(
    me_ref, x_hbm, w_hbm, ow_hbm, shift_ref, scale_ref,
    p0, p1, p2, p3, qkv_ref, own_ref, x_ref, w_ref, ow_ref, attended_ref, sems,
):
    x_copy, w_copy, ow_copy = fetch(
        (x_hbm, w_hbm.at[0], ow_hbm.at[0]), (x_ref, w_ref, ow_ref), sems
    )
    me = me_ref[0]
    x_copy.wait()
    tokens = x_ref[...]
    normed, _ = normalize(tokens)
    modded = (normed * (1.0 + scale_ref[0:1]) + shift_ref[0:1]).astype(BF16)
    modded = nn(order_matrix(0, 256), modded).astype(BF16)
    own_ref[...] = nn(order_matrix(me, ROWS), tokens).astype(BF16)
    w_copy.wait()
    queries, key_heads, value_heads = project(modded, w_ref[...])
    qkv_ref[0] = queries
    qkv_ref[1] = key_heads
    qkv_ref[2] = value_heads
    attended = []
    for queries_2, keys_2, values_2 in zip(pairs(queries), pairs(key_heads), pairs(value_heads)):
        total = jnp.zeros((256, GW // 2), F32)
        for head in range(2):
            probs = softmax(nt(of_head(queries_2, head), keys_2) * INV_ROOT)
            total = total + nn(probs.astype(BF16), of_head(values_2, head))
        attended.append(total)
    attended = jnp.concatenate(attended, axis=1)
    ow_copy.wait()
    attended_ref[...] = nn(attended.astype(BF16), ow_ref[...]).astype(BF16)
    for k, part in enumerate((p0, p1, p2, p3)):
        part[...] = attended_ref[chunk_rows((me + k) % 4), :]


def temporal(me_ref, m_ref, g_ref, w_ref, ow_ref, shift_ref, scale_ref, gate_ref, part_ref, out_part_ref):
    mid = m_ref[...]
    normed, _ = normalize(mid)
    modded = (normed * (1.0 + scale_ref[1:2]) + shift_ref[1:2]).astype(BF16)
    grad_proj = (gate_ref[1:2] * g_ref[...].astype(F32)).astype(BF16)
    queries, key_heads, value_heads = project(modded, w_ref[...])

    def spread(array):
        return jnp.concatenate([of_head(array, head) for head in range(HERE)], axis=0)

    def gather_heads(array):
        total = of_head(array[:ROWS], 0)
        for head in range(1, HERE):
            total = total + of_head(array[head * ROWS : (head + 1) * ROWS], head)
        return total

    queries_4 = spread(queries)
    probs = softmax(nt(queries_4, key_heads) * INV_ROOT)
    probs_low = probs.astype(BF16)
    grad_attn_4 = spread(nt(grad_proj, ow_ref[...]).astype(BF16))
    grad_probs = nt(grad_attn_4, value_heads)
    grad_scores = (
        probs * (grad_probs - jnp.sum(probs * grad_probs, axis=-1, keepdims=True)) * INV_ROOT
    ).astype(BF16)
    grad_query = gather_heads(nn(grad_scores, key_heads))
    grad_keys = tn(grad_scores, queries_4)
    grad_values = tn(probs_low, grad_attn_4)
    joined = jnp.concatenate([grad_query, grad_keys, grad_values], axis=1).astype(BF16)
    part_ref[...] = nn(joined, w_ref[...]).astype(BF16)
    attended = gather_heads(nn(probs_low, value_heads)).astype(BF16)
    out_part_ref[...] = nn(attended, ow_ref[...]).astype(BF16)


def spatial_backward(
    me_ref, grad_ref, qkv_ref, w_ref, ow_ref, gate_ref, p0, p1, p2, p3, total_ref
):
    grad = jnp.concatenate([grad_ref[chunk] for chunk in range(4)], axis=0)
    grad_proj = (gate_ref[0:1] * grad.astype(F32)).astype(BF16)
    grad_attn = nt(grad_proj, ow_ref[...]).astype(BF16)
    queries, key_heads, value_heads = qkv_ref[0], qkv_ref[1], qkv_ref[2]
    grads = []
    for queries_2, keys_2, values_2, grads_2 in zip(
        pairs(queries), pairs(key_heads), pairs(value_heads), pairs(grad_attn)
    ):
        grad_query = jnp.zeros((256, GW // 2), F32)
        grad_keys, grad_values = grad_query, grad_query
        for head in range(2):
            query = of_head(queries_2, head)
            grad_head = of_head(grads_2, head)
            probs = softmax(nt(query, keys_2) * INV_ROOT)
            grad_probs = nt(grad_head, values_2)
            grad_scores = (
                probs
                * (grad_probs - jnp.sum(probs * grad_probs, axis=-1, keepdims=True))
                * INV_ROOT
            ).astype(BF16)
            grad_query = grad_query + nn(grad_scores, of_head(keys_2, head))
            grad_keys = grad_keys + tn(grad_scores, query)
            grad_values = grad_values + tn(probs.astype(BF16), grad_head)
        grads.append((grad_query, grad_keys, grad_values))
    joined = jnp.concatenate([pair[i] for i in range(3) for pair in grads], axis=1).astype(BF16)
    total_ref[...] = nn(joined, w_ref[...]).astype(BF16)
    for k, part in enumerate((p0, p1, p2, p3)):
        part[...] = total_ref[chunk_rows((me_ref[0] + k) % 4), :]


def add_in(a_ref, b_ref, sum_ref):
    sum_ref[...] = a_ref[...].astype(F32) + b_ref[...].astype(F32)


def put(ref, rows):
    rows = rows.astype(ref.dtype)
    if len(ref.shape) == 3:
        ref[:, 0] = rows[:, : D // 2]
        ref[:, 1] = rows[:, D // 2 :]
    else:
        ref[...] = rows


def block_out(block, x_ref, gate_ref, *refs):
    total = refs[0][...].astype(F32)
    for ref in refs[1:-1]:
        total = total + ref[...].astype(F32)
    put(refs[-1], x_ref[...].astype(F32) + gate_ref[block : block + 1] * total)


def grad_of(block, x_ref, g_ref, scale_ref, *refs):
    total = refs[0][...].astype(F32)
    for ref in refs[1:-1]:
        total = total + ref[...].astype(F32)
    normed, inv_std = normalize(x_ref[...])
    grad = g_ref[...].astype(F32)
    back = norm_back(total, normed, inv_std, scale_ref[block : block + 1])
    put(refs[-1], grad + back)


def pack(grad_ref, result_ref, sent_ref):
    sent_ref[:ROWS] = jnp.concatenate([grad_ref[:, 0], grad_ref[:, 1]], axis=1)
    sent_ref[ROWS:] = result_ref[:HALF]


def pack_last(x_ref, g_ref, scale_ref, b0, b1, b2, b3, result_ref, sent_ref):
    grad_of(0, x_ref, g_ref, scale_ref, b0, b1, b2, b3, sent_ref.at[:ROWS])
    sent_ref[ROWS:] = result_ref[HALF:]


def unpack(first_ref, last_ref, ends_ref, result_ref, grad_ref):
    stacked = jnp.concatenate([ends_ref[chunk] for chunk in range(4)], axis=0)
    grad_ref[...] = tn(order_matrix(0, 256), stacked).astype(BF16)
    result_ref[:, :HALF] = first_ref[...]
    result_ref[:, HALF:] = last_ref[...]


IN_HBM = pl.BlockSpec(memory_space=pltpu.HBM)


def whole(shape):
    return pl.BlockSpec(shape, lambda *_: (0,) * len(shape))


QUARTER = whole((ROWS, D))
VECTORS = whole((2, D))
HALVES = jax.ShapeDtypeStruct((ROWS, 2, D // 2), BF16)


def rows_out(dtype=BF16):
    return jax.ShapeDtypeStruct((ROWS, D), dtype)


def run(
    body, me, operands, specs, out_shape, out_specs, flops,
    aliases=None, scratch=(), mib=24, moved=0,
):
    return pl.pallas_call(
        body,
        grid_spec=pltpu.PrefetchScalarGridSpec(
            num_scalar_prefetch=0 if me is None else 1,
            grid=(1,),
            in_specs=specs,
            out_specs=out_specs,
            scratch_shapes=list(scratch),
        ),
        out_shape=out_shape,
        input_output_aliases=aliases or {},
        compiler_params=pltpu.CompilerParams(vmem_limit_bytes=mib * 1024 * 1024),
        cost_estimate=pl.CostEstimate(flops=flops, bytes_accessed=moved, transcendentals=0),
    )(*(() if me is None else (me,)), *operands)


def shift(array, k):
    return lax.ppermute(array, "tp", [(i, (i + k) % N_TP) for i in range(N_TP)])


def across(array):
    return lax.all_to_all(array, "seq", split_axis=0, concat_axis=0, tiled=True)


def weights_of(block, weights, out_weight, after):
    weights, out_weight, _ = lax.optimization_barrier((weights, out_weight, after))
    return weights[block], out_weight[block]


def per_device(tokens, grad_out, qkv_weight, out_weight, mod_shift, mod_scale, mod_gate):
    me = lax.axis_index("tp").astype(jnp.int32).reshape(1)
    tokens = tokens.reshape(256, D)
    weights = jnp.transpose(qkv_weight, (0, 2, 3, 1)).reshape(2, 3 * GW, D)
    qkv_spec = whole((3, 256, GW))

    p0, p1, p2, p3, qkv_s, own = run(
        spatial_forward,
        me,
        (tokens, weights, out_weight, mod_shift, mod_scale),
        [IN_HBM, IN_HBM, IN_HBM, VECTORS, VECTORS],
        (rows_out(),) * 4 + (jax.ShapeDtypeStruct((3, 256, GW), BF16), rows_out()),
        (QUARTER,) * 4 + (qkv_spec, QUARTER),
        1_000_000_000,
        scratch=(
            pltpu.VMEM((256, D), BF16),
            pltpu.VMEM((3 * GW, D), BF16),
            pltpu.VMEM((GW, D), BF16),
            pltpu.VMEM((256, D), BF16),
            pltpu.SemaphoreType.DMA((3,)),
        ),
        mib=58,
    )
    p1, p3, p2 = shift(p1, 1), shift(p3, 3), shift(p2, 2)
    early = run(
        lambda *refs: block_out(0, *refs),
        None, (own, mod_gate, p0, p1), [QUARTER, VECTORS, QUARTER, QUARTER],
        rows_out(F32), QUARTER, 350_000_000,
    )
    middle = run(
        lambda *refs: block_out(0, *refs),
        None, (early, mod_gate, p3, p2), [QUARTER, VECTORS] + [QUARTER] * 2,
        HALVES, whole((ROWS, 2, D // 2)), 1_000_000,
    )
    mid_own = across(middle).reshape(ROWS, D)
    w_spec, ow_spec = whole((3 * GW, D)), whole((GW, D))
    w1, ow1 = weights_of(1, weights, out_weight, mid_own)

    mids = lax.all_gather(mid_own, "tp")
    sent, outs = {}, {}
    for k in (2, 1, 3, 0):
        chunk = pl.BlockSpec((None, ROWS, D), lambda _, at, k=k: ((at[0] + 4 - k) % 4, 0, 0))
        sent[k], outs[k] = run(
            temporal, me, (mids, grad_out, w1, ow1, mod_shift, mod_scale, mod_gate),
            [chunk, chunk, w_spec, ow_spec, VECTORS, VECTORS, VECTORS],
            (rows_out(), rows_out()), (QUARTER, QUARTER), 50_000_000 if k else 350_000_000,
        )
        if k:
            sent[k] = shift(sent[k], 4 - k)
    total = sent[0]
    for k in (2, 1):
        total = run(
            add_in, None, (total, sent[k]), [QUARTER] * 2, rows_out(F32), QUARTER, 350_000_000
        )
    outs = dict(zip(outs, lax.optimization_barrier(tuple(outs.values()))))
    for k in (2, 1, 3):
        outs[k] = shift(outs[k], 4 - k)
    result_own = run(
        lambda *refs: block_out(1, *refs),
        None, (mid_own, mod_gate, *(outs[k] for k in range(4))),
        [QUARTER, VECTORS] + [QUARTER] * 4, rows_out(), QUARTER, RESULT_FLOPS,
    )

    own_grad = pl.BlockSpec((None, ROWS, D), lambda _, at: (at[0], 0, 0))
    grad_patch = run(
        lambda me_ref, *refs: grad_of(1, *refs),
        me, (mid_own, grad_out, mod_scale, total, sent[3]),
        [QUARTER, own_grad, VECTORS] + [QUARTER] * 2,
        HALVES, whole((ROWS, 2, D // 2)), 1_000_000,
    )
    grad_own = across(grad_patch)
    w0, ow0 = weights_of(0, weights, out_weight, grad_own)
    message = jax.ShapeDtypeStruct((ROWS + HALF, D), BF16)
    packed = run(
        pack, None, (grad_own, result_own), [whole((ROWS, 2, D // 2)), QUARTER],
        message, whole((ROWS + HALF, D)), 1_000_000,
    )
    grads = lax.all_gather(packed, "tp")
    front, back = whole((4, ROWS, D)), pl.BlockSpec((4, HALF, D), lambda *_: (0, 2, 0))
    b0, b1, b2, b3 = run(
        spatial_backward, me, (grads, qkv_s, w0, ow0, mod_gate),
        [front, qkv_spec, w_spec, ow_spec, VECTORS],
        (rows_out(),) * 4, (QUARTER,) * 4, 1_500_000_000,
        scratch=(pltpu.VMEM((256, D), BF16),),
    )
    b1, b3, b2 = shift(b1, 1), shift(b3, 3), shift(b2, 2)
    packed = run(
        pack_last, None, (own, packed, mod_scale, b0, b1, b2, b3, result_own),
        [QUARTER] * 2 + [VECTORS] + [QUARTER] * 5,
        message, whole((ROWS + HALF, D)), 1_000_000,
    )
    ends = lax.all_gather(packed, "tp")
    result, grad_in = run(
        unpack, None, (grads, ends, ends), [back, back, front],
        (jax.ShapeDtypeStruct((4, ROWS, D), BF16), jax.ShapeDtypeStruct((256, D), BF16)),
        (whole((4, ROWS, D)), whole((256, D))), 100_000_000,
    )
    return (result, grad_in.reshape(256, 1, D))


def solution(mesh):
    in_specs = (
        P(None, "seq", None),
        P("seq", None, None),
        P(None, None, None, "tp"),
        P(None, "tp", None),
        P(),
        P(),
        P(),
    )
    out_specs = (P("seq", None, None), P(None, "seq", None))
    return jax.shard_map(
        per_device, mesh=mesh, in_specs=in_specs, out_specs=out_specs, check_vma=False
    )
```

```python
import functools
import math

import jax
import jax.numpy as jnp
from jax import lax
from jax.experimental import pallas as pl
from jax.experimental.pallas import tpu as pltpu
from jax.sharding import PartitionSpec as P

D = 1152
HEAD_DIM = 72
HERE = 4
GW = HERE * HEAD_DIM
N_TP = 4
ROWS = 64
HALF = 32
GROUPS = ((2,), (1,), (3,), (0,))
RESULT_FLOPS = 3_000_000_000
INV_ROOT = 1.0 / math.sqrt(HEAD_DIM)
F32 = jnp.float32
BF16 = jnp.bfloat16


def nn(a, b):
    return lax.dot_general(a, b, (((1,), (0,)), ((), ())), preferred_element_type=F32)


def nt(a, b):
    return lax.dot_general(a, b, (((1,), (1,)), ((), ())), preferred_element_type=F32)


def tn(a, b):
    return lax.dot_general(a, b, (((0,), (0,)), ((), ())), preferred_element_type=F32)


def normalize(tokens):
    widened = tokens.astype(F32)
    center = widened - jnp.mean(widened, axis=-1, keepdims=True)
    inv_std = lax.rsqrt(jnp.mean(center * center, axis=-1, keepdims=True) + 1e-06)
    return center * inv_std, inv_std


def norm_back(grad_mod, normed, inv_std, scale_row):
    grad_norm = grad_mod * (1.0 + scale_row)
    return inv_std * (
        grad_norm
        - jnp.mean(grad_norm, axis=-1, keepdims=True)
        - normed * jnp.mean(grad_norm * normed, axis=-1, keepdims=True)
    )


def softmax(scores):
    top = jnp.max(scores, axis=-1, keepdims=True)
    raised = jnp.exp(scores - top)
    return raised / jnp.sum(raised, axis=-1, keepdims=True)


def of_head(array, head):
    lane = lax.broadcasted_iota(jnp.int32, array.shape, 1)
    keep = (lane >= head * HEAD_DIM) & (lane < (head + 1) * HEAD_DIM)
    return jnp.where(keep, array, jnp.zeros_like(array))


def pairs(array):
    return array[:, : GW // 2], array[:, GW // 2 :]


def order_matrix(first, rows):
    place = lax.broadcasted_iota(jnp.int32, (rows, 256), 0)
    patch = lax.broadcasted_iota(jnp.int32, (rows, 256), 1)
    return (patch == 4 * (place % ROWS) + first + place // ROWS).astype(F32).astype(BF16)


def chunk_rows(chunk):
    return pl.ds(pl.multiple_of(chunk * ROWS, ROWS), ROWS)


def fetch(sources, buffers, sems):
    copies = [
        pltpu.make_async_copy(source, buffer, sems.at[i])
        for i, (source, buffer) in enumerate(zip(sources, buffers))
    ]
    for copy in copies:
        copy.start()
    return copies


def project(modded, weights):
    joined = nt(modded, weights)
    return tuple(joined[:, i * GW : (i + 1) * GW].astype(BF16) for i in range(3))


def spatial_forward(
    me_ref, x_hbm, w_hbm, ow_hbm, shift_ref, scale_ref,
    p0, p1, p2, p3, qkv_ref, own_ref, x_ref, w_ref, ow_ref, attended_ref, sems,
):
    x_copy, w_copy, ow_copy = fetch(
        (x_hbm, w_hbm.at[0], ow_hbm.at[0]), (x_ref, w_ref, ow_ref), sems
    )
    me = me_ref[0]
    x_copy.wait()
    tokens = x_ref[...]
    normed, _ = normalize(tokens)
    modded = (normed * (1.0 + scale_ref[0:1]) + shift_ref[0:1]).astype(BF16)
    modded = nn(order_matrix(0, 256), modded).astype(BF16)
    own_ref[...] = nn(order_matrix(me, ROWS), tokens).astype(BF16)
    w_copy.wait()
    queries, key_heads, value_heads = project(modded, w_ref[...])
    qkv_ref[0] = queries
    qkv_ref[1] = key_heads
    qkv_ref[2] = value_heads
    attended = []
    for queries_2, keys_2, values_2 in zip(pairs(queries), pairs(key_heads), pairs(value_heads)):
        total = jnp.zeros((256, GW // 2), F32)
        for head in range(2):
            probs = softmax(nt(of_head(queries_2, head), keys_2) * INV_ROOT)
            total = total + nn(probs.astype(BF16), of_head(values_2, head))
        attended.append(total)
    attended = jnp.concatenate(attended, axis=1)
    ow_copy.wait()
    attended_ref[...] = nn(attended.astype(BF16), ow_ref[...]).astype(BF16)
    for k, part in enumerate((p0, p1, p2, p3)):
        part[...] = attended_ref[chunk_rows((me + k) % 4), :]


def temporal(count, me_ref, *refs):
    mids, grads = refs[:count], refs[count : 2 * count]
    w_ref, ow_ref, shift_ref, scale_ref, gate_ref = refs[2 * count : 2 * count + 5]
    part_refs, out_refs = refs[2 * count + 5 : 3 * count + 5], refs[3 * count + 5 :]

    def rows_of(array, i):
        return array[i * ROWS : (i + 1) * ROWS]

    def stack(pieces):
        return jnp.concatenate(pieces, axis=0) if len(pieces) > 1 else pieces[0]

    def spread(array):
        return jnp.concatenate([of_head(array, head) for head in range(HERE)], axis=0)

    def gather_heads(array):
        total = of_head(array[:ROWS], 0)
        for head in range(1, HERE):
            total = total + of_head(rows_of(array, head), head)
        return total

    normed, _ = normalize(stack([ref[...] for ref in mids]))
    modded = (normed * (1.0 + scale_ref[1:2]) + shift_ref[1:2]).astype(BF16)
    grad = stack([ref[...] for ref in grads]).astype(F32)
    grad_proj = (gate_ref[1:2] * grad).astype(BF16)
    queries, key_heads, value_heads = project(modded, w_ref[...])
    grad_attn = nt(grad_proj, ow_ref[...]).astype(BF16)
    joined, attended = [], []
    for i in range(count):
        keys_i, values_i = rows_of(key_heads, i), rows_of(value_heads, i)
        queries_4 = spread(rows_of(queries, i))
        probs = softmax(nt(queries_4, keys_i) * INV_ROOT)
        probs_low = probs.astype(BF16)
        grad_attn_4 = spread(rows_of(grad_attn, i))
        grad_probs = nt(grad_attn_4, values_i)
        grad_scores = (
            probs * (grad_probs - jnp.sum(probs * grad_probs, axis=-1, keepdims=True)) * INV_ROOT
        ).astype(BF16)
        grad_query = gather_heads(nn(grad_scores, keys_i))
        grad_keys = tn(grad_scores, queries_4)
        grad_values = tn(probs_low, grad_attn_4)
        joined.append(
            jnp.concatenate([grad_query, grad_keys, grad_values], axis=1).astype(BF16)
        )
        attended.append(gather_heads(nn(probs_low, values_i)).astype(BF16))
    part = nn(stack(joined), w_ref[...]).astype(BF16)
    out = nn(stack(attended), ow_ref[...]).astype(BF16)
    for i in range(count):
        part_refs[i][...] = rows_of(part, i)
        out_refs[i][...] = rows_of(out, i)


def spatial_backward(
    me_ref, grad_ref, qkv_ref, w_ref, ow_ref, gate_ref, p0, p1, p2, p3, total_ref
):
    grad = jnp.concatenate([grad_ref[chunk] for chunk in range(4)], axis=0)
    grad_proj = (gate_ref[0:1] * grad.astype(F32)).astype(BF16)
    grad_attn = nt(grad_proj, ow_ref[...]).astype(BF16)
    queries, key_heads, value_heads = qkv_ref[0], qkv_ref[1], qkv_ref[2]
    grads = []
    for queries_2, keys_2, values_2, grads_2 in zip(
        pairs(queries), pairs(key_heads), pairs(value_heads), pairs(grad_attn)
    ):
        grad_query = jnp.zeros((256, GW // 2), F32)
        grad_keys, grad_values = grad_query, grad_query
        for head in range(2):
            query = of_head(queries_2, head)
            grad_head = of_head(grads_2, head)
            probs = softmax(nt(query, keys_2) * INV_ROOT)
            grad_probs = nt(grad_head, values_2)
            grad_scores = (
                probs
                * (grad_probs - jnp.sum(probs * grad_probs, axis=-1, keepdims=True))
                * INV_ROOT
            ).astype(BF16)
            grad_query = grad_query + nn(grad_scores, of_head(keys_2, head))
            grad_keys = grad_keys + tn(grad_scores, query)
            grad_values = grad_values + tn(probs.astype(BF16), grad_head)
        grads.append((grad_query, grad_keys, grad_values))
    joined = jnp.concatenate([pair[i] for i in range(3) for pair in grads], axis=1).astype(BF16)
    total_ref[...] = nn(joined, w_ref[...]).astype(BF16)
    for k, part in enumerate((p0, p1, p2, p3)):
        part[...] = total_ref[chunk_rows((me_ref[0] + k) % 4), :]


def add_in(a_ref, b_ref, sum_ref):
    sum_ref[...] = a_ref[...].astype(F32) + b_ref[...].astype(F32)


def put(ref, rows):
    rows = rows.astype(ref.dtype)
    if len(ref.shape) == 3:
        ref[:, 0] = rows[:, : D // 2]
        ref[:, 1] = rows[:, D // 2 :]
    else:
        ref[...] = rows


def block_out(block, x_ref, gate_ref, *refs):
    total = refs[0][...].astype(F32)
    for ref in refs[1:-1]:
        total = total + ref[...].astype(F32)
    put(refs[-1], x_ref[...].astype(F32) + gate_ref[block : block + 1] * total)


def grad_of(block, x_ref, g_ref, scale_ref, *refs):
    total = refs[0][...].astype(F32)
    for ref in refs[1:-1]:
        total = total + ref[...].astype(F32)
    normed, inv_std = normalize(x_ref[...])
    grad = g_ref[...].astype(F32)
    back = norm_back(total, normed, inv_std, scale_ref[block : block + 1])
    put(refs[-1], grad + back)


def pack(grad_ref, result_ref, sent_ref):
    sent_ref[:ROWS] = jnp.concatenate([grad_ref[:, 0], grad_ref[:, 1]], axis=1)
    sent_ref[ROWS:] = result_ref[:HALF]


def pack_last(x_ref, g_ref, scale_ref, b0, b1, b2, b3, result_ref, sent_ref):
    grad_of(0, x_ref, g_ref, scale_ref, b0, b1, b2, b3, sent_ref.at[:ROWS])
    sent_ref[ROWS:] = result_ref[HALF:]


def unpack(first_ref, last_ref, ends_ref, result_ref, grad_ref):
    stacked = jnp.concatenate([ends_ref[chunk] for chunk in range(4)], axis=0)
    grad_ref[...] = tn(order_matrix(0, 256), stacked).astype(BF16)
    result_ref[:, :HALF] = first_ref[...]
    result_ref[:, HALF:] = last_ref[...]


IN_HBM = pl.BlockSpec(memory_space=pltpu.HBM)


def whole(shape):
    return pl.BlockSpec(shape, lambda *_: (0,) * len(shape))


QUARTER = whole((ROWS, D))
VECTORS = whole((2, D))
HALVES = jax.ShapeDtypeStruct((ROWS, 2, D // 2), BF16)


def rows_out(dtype=BF16):
    return jax.ShapeDtypeStruct((ROWS, D), dtype)


def run(
    body, me, operands, specs, out_shape, out_specs, flops,
    aliases=None, scratch=(), mib=24, moved=0,
):
    return pl.pallas_call(
        body,
        grid_spec=pltpu.PrefetchScalarGridSpec(
            num_scalar_prefetch=0 if me is None else 1,
            grid=(1,),
            in_specs=specs,
            out_specs=out_specs,
            scratch_shapes=list(scratch),
        ),
        out_shape=out_shape,
        input_output_aliases=aliases or {},
        compiler_params=pltpu.CompilerParams(vmem_limit_bytes=mib * 1024 * 1024),
        cost_estimate=pl.CostEstimate(flops=flops, bytes_accessed=moved, transcendentals=0),
    )(*(() if me is None else (me,)), *operands)


def shift(array, k):
    return lax.ppermute(array, "tp", [(i, (i + k) % N_TP) for i in range(N_TP)])


def across(array):
    return lax.all_to_all(array, "seq", split_axis=0, concat_axis=0, tiled=True)


def weights_of(block, weights, out_weight, after):
    weights, out_weight, _ = lax.optimization_barrier((weights, out_weight, after))
    return weights[block], out_weight[block]


def per_device(tokens, grad_out, qkv_weight, out_weight, mod_shift, mod_scale, mod_gate):
    me = lax.axis_index("tp").astype(jnp.int32).reshape(1)
    tokens = tokens.reshape(256, D)
    weights = jnp.transpose(qkv_weight, (0, 2, 3, 1)).reshape(2, 3 * GW, D)
    qkv_spec = whole((3, 256, GW))

    p0, p1, p2, p3, qkv_s, own = run(
        spatial_forward,
        me,
        (tokens, weights, out_weight, mod_shift, mod_scale),
        [IN_HBM, IN_HBM, IN_HBM, VECTORS, VECTORS],
        (rows_out(),) * 4 + (jax.ShapeDtypeStruct((3, 256, GW), BF16), rows_out()),
        (QUARTER,) * 4 + (qkv_spec, QUARTER),
        1_000_000_000,
        scratch=(
            pltpu.VMEM((256, D), BF16),
            pltpu.VMEM((3 * GW, D), BF16),
            pltpu.VMEM((GW, D), BF16),
            pltpu.VMEM((256, D), BF16),
            pltpu.SemaphoreType.DMA((3,)),
        ),
        mib=58,
    )
    p1, p3, p2 = shift(p1, 1), shift(p3, 3), shift(p2, 2)
    early = run(
        lambda *refs: block_out(0, *refs),
        None, (own, mod_gate, p0, p1), [QUARTER, VECTORS, QUARTER, QUARTER],
        rows_out(F32), QUARTER, 350_000_000,
    )
    middle = run(
        lambda *refs: block_out(0, *refs),
        None, (early, mod_gate, p3, p2), [QUARTER, VECTORS] + [QUARTER] * 2,
        HALVES, whole((ROWS, 2, D // 2)), 1_000_000,
    )
    mid_own = across(middle).reshape(ROWS, D)
    w_spec, ow_spec = whole((3 * GW, D)), whole((GW, D))
    w1, ow1 = weights_of(1, weights, out_weight, mid_own)

    mids = lax.all_gather(mid_own, "tp")
    sent, outs = {}, {}
    for group in GROUPS:
        chunks = [
            pl.BlockSpec((None, ROWS, D), lambda _, at, k=k: ((at[0] + 4 - k) % 4, 0, 0))
            for k in group
        ]
        count = len(group)
        made = run(
            functools.partial(temporal, count), me,
            (mids,) * count + (grad_out,) * count + (w1, ow1, mod_shift, mod_scale, mod_gate),
            chunks * 2 + [w_spec, ow_spec, VECTORS, VECTORS, VECTORS],
            (rows_out(),) * (2 * count), (QUARTER,) * (2 * count),
            50_000_000 if group[-1] else 350_000_000,
        )
        for i, k in enumerate(group):
            sent[k] = shift(made[i], 4 - k) if k else made[i]
            outs[k] = made[count + i]
    total = sent[0]
    for k in (2, 1):
        total = run(
            add_in, None, (total, sent[k]), [QUARTER] * 2, rows_out(F32), QUARTER, 350_000_000
        )
    outs = dict(zip(outs, lax.optimization_barrier(tuple(outs.values()))))
    for k in (2, 1, 3):
        outs[k] = shift(outs[k], 4 - k)
    result_own = run(
        lambda *refs: block_out(1, *refs),
        None, (mid_own, mod_gate, *(outs[k] for k in range(4))),
        [QUARTER, VECTORS] + [QUARTER] * 4, rows_out(), QUARTER, RESULT_FLOPS,
    )

    own_grad = pl.BlockSpec((None, ROWS, D), lambda _, at: (at[0], 0, 0))
    grad_patch = run(
        lambda me_ref, *refs: grad_of(1, *refs),
        me, (mid_own, grad_out, mod_scale, total, sent[3]),
        [QUARTER, own_grad, VECTORS] + [QUARTER] * 2,
        HALVES, whole((ROWS, 2, D // 2)), 1_000_000,
    )
    grad_own = across(grad_patch)
    w0, ow0 = weights_of(0, weights, out_weight, grad_own)
    message = jax.ShapeDtypeStruct((ROWS + HALF, D), BF16)
    packed = run(
        pack, None, (grad_own, result_own), [whole((ROWS, 2, D // 2)), QUARTER],
        message, whole((ROWS + HALF, D)), 1_000_000,
    )
    grads = lax.all_gather(packed, "tp")
    front, back = whole((4, ROWS, D)), pl.BlockSpec((4, HALF, D), lambda *_: (0, 2, 0))
    b0, b1, b2, b3 = run(
        spatial_backward, me, (grads, qkv_s, w0, ow0, mod_gate),
        [front, qkv_spec, w_spec, ow_spec, VECTORS],
        (rows_out(),) * 4, (QUARTER,) * 4, 1_500_000_000,
        scratch=(pltpu.VMEM((256, D), BF16),),
    )
    b1, b3, b2 = shift(b1, 1), shift(b3, 3), shift(b2, 2)
    packed = run(
        pack_last, None, (own, packed, mod_scale, b0, b1, b2, b3, result_own),
        [QUARTER] * 2 + [VECTORS] + [QUARTER] * 5,
        message, whole((ROWS + HALF, D)), 1_000_000,
    )
    ends = lax.all_gather(packed, "tp")
    result, grad_in = run(
        unpack, None, (grads, ends, ends), [back, back, front],
        (jax.ShapeDtypeStruct((4, ROWS, D), BF16), jax.ShapeDtypeStruct((256, D), BF16)),
        (whole((4, ROWS, D)), whole((256, D))), 100_000_000,
    )
    return (result, grad_in.reshape(256, 1, D))


def solution(mesh):
    in_specs = (
        P(None, "seq", None),
        P("seq", None, None),
        P(None, None, None, "tp"),
        P(None, "tp", None),
        P(),
        P(),
        P(),
    )
    out_specs = (P("seq", None, None), P(None, "seq", None))
    return jax.shard_map(
        per_device, mesh=mesh, in_specs=in_specs, out_specs=out_specs, check_vma=False
    )
```

```python
import functools
import math

import jax
import jax.numpy as jnp
from jax import lax
from jax.experimental import pallas as pl
from jax.experimental.pallas import tpu as pltpu
from jax.sharding import PartitionSpec as P

D = 1152
HEAD_DIM = 72
HERE = 4
GW = HERE * HEAD_DIM
N_TP = 4
ROWS = 64
HALF = 32
GROUPS = ((2,), (1,), (3,), (0,))
RESULT_FLOPS = 3_000_000_000
INV_ROOT = 1.0 / math.sqrt(HEAD_DIM)
F32 = jnp.float32
BF16 = jnp.bfloat16


def nn(a, b):
    return lax.dot_general(a, b, (((1,), (0,)), ((), ())), preferred_element_type=F32)


def nt(a, b):
    return lax.dot_general(a, b, (((1,), (1,)), ((), ())), preferred_element_type=F32)


def tn(a, b):
    return lax.dot_general(a, b, (((0,), (0,)), ((), ())), preferred_element_type=F32)


def normalize(tokens):
    widened = tokens.astype(F32)
    center = widened - jnp.mean(widened, axis=-1, keepdims=True)
    inv_std = lax.rsqrt(jnp.mean(center * center, axis=-1, keepdims=True) + 1e-06)
    return center * inv_std, inv_std


def norm_back(grad_mod, normed, inv_std, scale_row):
    grad_norm = grad_mod * (1.0 + scale_row)
    return inv_std * (
        grad_norm
        - jnp.mean(grad_norm, axis=-1, keepdims=True)
        - normed * jnp.mean(grad_norm * normed, axis=-1, keepdims=True)
    )


def softmax(scores):
    top = jnp.max(scores, axis=-1, keepdims=True)
    raised = jnp.exp(scores - top)
    return raised / jnp.sum(raised, axis=-1, keepdims=True)


def of_head(array, head):
    lane = lax.broadcasted_iota(jnp.int32, array.shape, 1)
    keep = (lane >= head * HEAD_DIM) & (lane < (head + 1) * HEAD_DIM)
    return jnp.where(keep, array, jnp.zeros_like(array))


def pairs(array):
    return array[:, : GW // 2], array[:, GW // 2 :]


def order_matrix(first, rows):
    place = lax.broadcasted_iota(jnp.int32, (rows, 256), 0)
    patch = lax.broadcasted_iota(jnp.int32, (rows, 256), 1)
    return (patch == 4 * (place % ROWS) + first + place // ROWS).astype(F32).astype(BF16)


def chunk_rows(chunk):
    return pl.ds(pl.multiple_of(chunk * ROWS, ROWS), ROWS)


def fetch(sources, buffers, sems):
    copies = [
        pltpu.make_async_copy(source, buffer, sems.at[i])
        for i, (source, buffer) in enumerate(zip(sources, buffers))
    ]
    for copy in copies:
        copy.start()
    return copies


def project(modded, weights):
    joined = nt(modded, weights)
    return tuple(joined[:, i * GW : (i + 1) * GW].astype(BF16) for i in range(3))


def spatial_forward(
    me_ref, x_hbm, w_hbm, ow_hbm, shift_ref, scale_ref,
    p0, p1, p2, p3, qkv_ref, own_ref, x_ref, w_ref, ow_ref, attended_ref, sems,
):
    x_copy, w_copy, ow_copy = fetch(
        (x_hbm, w_hbm.at[0], ow_hbm.at[0]), (x_ref, w_ref, ow_ref), sems
    )
    me = me_ref[0]
    x_copy.wait()
    tokens = x_ref[...]
    normed, _ = normalize(tokens)
    modded = (normed * (1.0 + scale_ref[0:1]) + shift_ref[0:1]).astype(BF16)
    modded = nn(order_matrix(0, 256), modded).astype(BF16)
    own_ref[...] = nn(order_matrix(me, ROWS), tokens).astype(BF16)
    w_copy.wait()
    queries, key_heads, value_heads = project(modded, w_ref[...])
    qkv_ref[0] = queries
    qkv_ref[1] = key_heads
    qkv_ref[2] = value_heads
    attended = []
    for queries_2, keys_2, values_2 in zip(pairs(queries), pairs(key_heads), pairs(value_heads)):
        total = jnp.zeros((256, GW // 2), F32)
        for head in range(2):
            probs = softmax(nt(of_head(queries_2, head), keys_2) * INV_ROOT)
            total = total + nn(probs.astype(BF16), of_head(values_2, head))
        attended.append(total)
    attended = jnp.concatenate(attended, axis=1)
    ow_copy.wait()
    attended_ref[...] = nn(attended.astype(BF16), ow_ref[...]).astype(BF16)
    for k, part in enumerate((p0, p1, p2, p3)):
        part[...] = attended_ref[chunk_rows((me + k) % 4), :]


def temporal(count, me_ref, *refs):
    mids, grads = refs[:count], refs[count : 2 * count]
    w_ref, ow_ref, shift_ref, scale_ref, gate_ref = refs[2 * count : 2 * count + 5]
    part_refs, out_refs = refs[2 * count + 5 : 3 * count + 5], refs[3 * count + 5 :]

    def rows_of(array, i):
        return array[i * ROWS : (i + 1) * ROWS]

    def stack(pieces):
        return jnp.concatenate(pieces, axis=0) if len(pieces) > 1 else pieces[0]

    def spread(array):
        return jnp.concatenate([of_head(array, head) for head in range(HERE)], axis=0)

    def gather_heads(array):
        total = of_head(array[:ROWS], 0)
        for head in range(1, HERE):
            total = total + of_head(rows_of(array, head), head)
        return total

    normed, _ = normalize(stack([ref[...] for ref in mids]))
    modded = (normed * (1.0 + scale_ref[1:2]) + shift_ref[1:2]).astype(BF16)
    grad = stack([ref[...] for ref in grads]).astype(F32)
    grad_proj = (gate_ref[1:2] * grad).astype(BF16)
    queries, key_heads, value_heads = project(modded, w_ref[...])
    grad_attn = nt(grad_proj, ow_ref[...]).astype(BF16)
    joined, attended = [], []
    for i in range(count):
        keys_i, values_i = rows_of(key_heads, i), rows_of(value_heads, i)
        queries_4 = spread(rows_of(queries, i))
        probs = softmax(nt(queries_4, keys_i) * INV_ROOT)
        probs_low = probs.astype(BF16)
        grad_attn_4 = spread(rows_of(grad_attn, i))
        grad_probs = nt(grad_attn_4, values_i)
        grad_scores = (
            probs * (grad_probs - jnp.sum(probs * grad_probs, axis=-1, keepdims=True)) * INV_ROOT
        ).astype(BF16)
        grad_query = gather_heads(nn(grad_scores, keys_i))
        grad_keys = tn(grad_scores, queries_4)
        grad_values = tn(probs_low, grad_attn_4)
        joined.append(
            jnp.concatenate([grad_query, grad_keys, grad_values], axis=1).astype(BF16)
        )
        attended.append(gather_heads(nn(probs_low, values_i)).astype(BF16))
    part = nn(stack(joined), w_ref[...]).astype(BF16)
    out = nn(stack(attended), ow_ref[...]).astype(BF16)
    for i in range(count):
        part_refs[i][...] = rows_of(part, i)
        out_refs[i][...] = rows_of(out, i)


def spatial_backward(
    me_ref, grad_ref, qkv_ref, w_ref, ow_ref, gate_ref, p0, p1, p2, p3, total_ref
):
    grad = jnp.concatenate([grad_ref[chunk] for chunk in range(4)], axis=0)
    grad_proj = (gate_ref[0:1] * grad.astype(F32)).astype(BF16)
    grad_attn = nt(grad_proj, ow_ref[...]).astype(BF16)
    queries, key_heads, value_heads = qkv_ref[0], qkv_ref[1], qkv_ref[2]
    grads = []
    for queries_2, keys_2, values_2, grads_2 in zip(
        pairs(queries), pairs(key_heads), pairs(value_heads), pairs(grad_attn)
    ):
        grad_query = jnp.zeros((256, GW // 2), F32)
        grad_keys, grad_values = grad_query, grad_query
        for head in range(2):
            query = of_head(queries_2, head)
            grad_head = of_head(grads_2, head)
            probs = softmax(nt(query, keys_2) * INV_ROOT)
            grad_probs = nt(grad_head, values_2)
            grad_scores = (
                probs
                * (grad_probs - jnp.sum(probs * grad_probs, axis=-1, keepdims=True))
                * INV_ROOT
            ).astype(BF16)
            grad_query = grad_query + nn(grad_scores, of_head(keys_2, head))
            grad_keys = grad_keys + tn(grad_scores, query)
            grad_values = grad_values + tn(probs.astype(BF16), grad_head)
        grads.append((grad_query, grad_keys, grad_values))
    joined = jnp.concatenate([pair[i] for i in range(3) for pair in grads], axis=1).astype(BF16)
    total_ref[...] = nn(joined, w_ref[...]).astype(BF16)
    for k, part in enumerate((p0, p1, p2, p3)):
        part[...] = total_ref[chunk_rows((me_ref[0] + k) % 4), :]


def add_in(a_ref, b_ref, sum_ref):
    sum_ref[...] = a_ref[...].astype(F32) + b_ref[...].astype(F32)


def put(ref, rows):
    rows = rows.astype(ref.dtype)
    if len(ref.shape) == 3:
        ref[:, 0] = rows[:, : D // 2]
        ref[:, 1] = rows[:, D // 2 :]
    else:
        ref[...] = rows


def block_out(block, x_ref, gate_ref, *refs):
    total = refs[0][...].astype(F32)
    for ref in refs[1:-1]:
        total = total + ref[...].astype(F32)
    put(refs[-1], x_ref[...].astype(F32) + gate_ref[block : block + 1] * total)


def grad_of(block, x_ref, g_ref, scale_ref, *refs):
    total = refs[0][...].astype(F32)
    for ref in refs[1:-1]:
        total = total + ref[...].astype(F32)
    normed, inv_std = normalize(x_ref[...])
    grad = g_ref[...].astype(F32)
    back = norm_back(total, normed, inv_std, scale_ref[block : block + 1])
    put(refs[-1], grad + back)


def pack(grad_ref, result_ref, sent_ref):
    sent_ref[:ROWS] = jnp.concatenate([grad_ref[:, 0], grad_ref[:, 1]], axis=1)
    sent_ref[ROWS:] = result_ref[:HALF]


def pack_last(x_ref, g_ref, scale_ref, early, b3, b2, result_ref, sent_ref):
    grad_of(0, x_ref, g_ref, scale_ref, early, b3, b2, sent_ref.at[:ROWS])
    sent_ref[ROWS:] = result_ref[HALF:]


def unpack(first_ref, last_ref, ends_ref, result_ref, grad_ref):
    stacked = jnp.concatenate([ends_ref[chunk] for chunk in range(4)], axis=0)
    patch = lax.broadcasted_iota(jnp.int32, (256, 256), 0)
    place = lax.broadcasted_iota(jnp.int32, (256, 256), 1)
    order = (patch == 4 * (place % ROWS) + place // ROWS).astype(F32).astype(BF16)
    grad_ref[...] = nn(order, stacked).astype(BF16)
    result_ref[:, :HALF] = first_ref[...]
    result_ref[:, HALF:] = last_ref[...]


IN_HBM = pl.BlockSpec(memory_space=pltpu.HBM)


def whole(shape):
    return pl.BlockSpec(shape, lambda *_: (0,) * len(shape))


QUARTER = whole((ROWS, D))
VECTORS = whole((2, D))
HALVES = jax.ShapeDtypeStruct((ROWS, 2, D // 2), BF16)


def rows_out(dtype=BF16):
    return jax.ShapeDtypeStruct((ROWS, D), dtype)


def run(
    body, me, operands, specs, out_shape, out_specs, flops,
    aliases=None, scratch=(), mib=24, moved=0,
):
    return pl.pallas_call(
        body,
        grid_spec=pltpu.PrefetchScalarGridSpec(
            num_scalar_prefetch=0 if me is None else 1,
            grid=(1,),
            in_specs=specs,
            out_specs=out_specs,
            scratch_shapes=list(scratch),
        ),
        out_shape=out_shape,
        input_output_aliases=aliases or {},
        compiler_params=pltpu.CompilerParams(vmem_limit_bytes=mib * 1024 * 1024),
        cost_estimate=pl.CostEstimate(flops=flops, bytes_accessed=moved, transcendentals=0),
    )(*(() if me is None else (me,)), *operands)


def shift(array, k):
    return lax.ppermute(array, "tp", [(i, (i + k) % N_TP) for i in range(N_TP)])


def across(array):
    return lax.all_to_all(array, "seq", split_axis=0, concat_axis=0, tiled=True)


def weights_of(block, weights, out_weight, after):
    weights, out_weight, _ = lax.optimization_barrier((weights, out_weight, after))
    return weights[block], out_weight[block]


def per_device(tokens, grad_out, qkv_weight, out_weight, mod_shift, mod_scale, mod_gate):
    me = lax.axis_index("tp").astype(jnp.int32).reshape(1)
    tokens = tokens.reshape(256, D)
    weights = jnp.transpose(qkv_weight, (0, 2, 3, 1)).reshape(2, 3 * GW, D)
    qkv_spec = whole((3, 256, GW))

    p0, p1, p2, p3, qkv_s, own = run(
        spatial_forward,
        me,
        (tokens, weights, out_weight, mod_shift, mod_scale),
        [IN_HBM, IN_HBM, IN_HBM, VECTORS, VECTORS],
        (rows_out(),) * 4 + (jax.ShapeDtypeStruct((3, 256, GW), BF16), rows_out()),
        (QUARTER,) * 4 + (qkv_spec, QUARTER),
        1_000_000_000,
        scratch=(
            pltpu.VMEM((256, D), BF16),
            pltpu.VMEM((3 * GW, D), BF16),
            pltpu.VMEM((GW, D), BF16),
            pltpu.VMEM((256, D), BF16),
            pltpu.SemaphoreType.DMA((3,)),
        ),
        mib=58,
    )
    p1, p3, p2 = shift(p1, 1), shift(p3, 3), shift(p2, 2)
    early = run(
        lambda *refs: block_out(0, *refs),
        None, (own, mod_gate, p0, p1), [QUARTER, VECTORS, QUARTER, QUARTER],
        rows_out(F32), QUARTER, 350_000_000,
    )
    middle = run(
        lambda *refs: block_out(0, *refs),
        None, (early, mod_gate, p3, p2), [QUARTER, VECTORS] + [QUARTER] * 2,
        HALVES, whole((ROWS, 2, D // 2)), 1_000_000,
    )
    mid_own = across(middle).reshape(ROWS, D)
    w_spec, ow_spec = whole((3 * GW, D)), whole((GW, D))
    w1, ow1 = weights_of(1, weights, out_weight, mid_own)

    mids = lax.all_gather(mid_own, "tp")
    sent, outs = {}, {}
    for group in GROUPS:
        chunks = [
            pl.BlockSpec((None, ROWS, D), lambda _, at, k=k: ((at[0] + 4 - k) % 4, 0, 0))
            for k in group
        ]
        count = len(group)
        made = run(
            functools.partial(temporal, count), me,
            (mids,) * count + (grad_out,) * count + (w1, ow1, mod_shift, mod_scale, mod_gate),
            chunks * 2 + [w_spec, ow_spec, VECTORS, VECTORS, VECTORS],
            (rows_out(),) * (2 * count), (QUARTER,) * (2 * count),
            50_000_000 if group[-1] else 350_000_000,
        )
        for i, k in enumerate(group):
            sent[k] = shift(made[i], 4 - k) if k else made[i]
            outs[k] = made[count + i]
    total = sent[0]
    for k in (2, 1):
        total = run(
            add_in, None, (total, sent[k]), [QUARTER] * 2, rows_out(F32), QUARTER, 350_000_000
        )
    outs = dict(zip(outs, lax.optimization_barrier(tuple(outs.values()))))
    for k in (2, 1, 3):
        outs[k] = shift(outs[k], 4 - k)
    result_own = run(
        lambda *refs: block_out(1, *refs),
        None, (mid_own, mod_gate, *(outs[k] for k in range(4))),
        [QUARTER, VECTORS] + [QUARTER] * 4, rows_out(), QUARTER, RESULT_FLOPS,
    )

    own_grad = pl.BlockSpec((None, ROWS, D), lambda _, at: (at[0], 0, 0))
    grad_patch = run(
        lambda me_ref, *refs: grad_of(1, *refs),
        me, (mid_own, grad_out, mod_scale, total, sent[3]),
        [QUARTER, own_grad, VECTORS] + [QUARTER] * 2,
        HALVES, whole((ROWS, 2, D // 2)), 1_000_000,
    )
    grad_own = across(grad_patch)
    w0, ow0 = weights_of(0, weights, out_weight, grad_own)
    message = jax.ShapeDtypeStruct((ROWS + HALF, D), BF16)
    packed = run(
        pack, None, (grad_own, result_own), [whole((ROWS, 2, D // 2)), QUARTER],
        message, whole((ROWS + HALF, D)), 1_000_000,
    )
    grads = lax.all_gather(packed, "tp")
    front, back = whole((4, ROWS, D)), pl.BlockSpec((4, HALF, D), lambda *_: (0, 2, 0))
    b0, b1, b2, b3 = run(
        spatial_backward, me, (grads, qkv_s, w0, ow0, mod_gate),
        [front, qkv_spec, w_spec, ow_spec, VECTORS],
        (rows_out(),) * 4, (QUARTER,) * 4, 1_500_000_000,
        scratch=(pltpu.VMEM((256, D), BF16),),
    )
    b1, b3, b2 = shift(b1, 1), shift(b3, 3), shift(b2, 2)
    early = run(add_in, None, (b0, b2), [QUARTER] * 2, rows_out(F32), QUARTER, 350_000_000)
    packed = run(
        pack_last, None, (own, packed, mod_scale, early, b1, b3, result_own),
        [QUARTER] * 2 + [VECTORS] + [QUARTER] * 4,
        message, whole((ROWS + HALF, D)), 1_000_000,
    )
    ends = lax.all_gather(packed, "tp")
    result, grad_in = run(
        unpack, None, (grads, ends, ends), [back, back, front],
        (jax.ShapeDtypeStruct((4, ROWS, D), BF16), jax.ShapeDtypeStruct((256, D), BF16)),
        (whole((4, ROWS, D)), whole((256, D))), 100_000_000,
    )
    return (result, grad_in.reshape(256, 1, D))


def solution(mesh):
    in_specs = (
        P(None, "seq", None),
        P("seq", None, None),
        P(None, None, None, "tp"),
        P(None, "tp", None),
        P(),
        P(),
        P(),
    )
    out_specs = (P("seq", None, None), P(None, "seq", None))
    return jax.shard_map(
        per_device, mesh=mesh, in_specs=in_specs, out_specs=out_specs, check_vma=False
    )
```

```python
import functools
import math

import jax
import jax.numpy as jnp
from jax import lax
from jax.experimental import pallas as pl
from jax.experimental.pallas import tpu as pltpu
from jax.sharding import PartitionSpec as P

D = 1152
HEAD_DIM = 72
HERE = 4
GW = HERE * HEAD_DIM
N_TP = 4
ROWS = 64
HALF = 32
GROUPS = ((2,), (1,), (3,), (0,))
RESULT_FLOPS = 3_000_000_000
INV_ROOT = 1.0 / math.sqrt(HEAD_DIM)
F32 = jnp.float32
BF16 = jnp.bfloat16


def nn(a, b):
    return lax.dot_general(a, b, (((1,), (0,)), ((), ())), preferred_element_type=F32)


def nt(a, b):
    return lax.dot_general(a, b, (((1,), (1,)), ((), ())), preferred_element_type=F32)


def tn(a, b):
    return lax.dot_general(a, b, (((0,), (0,)), ((), ())), preferred_element_type=F32)


def normalize(tokens):
    widened = tokens.astype(F32)
    center = widened - jnp.mean(widened, axis=-1, keepdims=True)
    inv_std = lax.rsqrt(jnp.mean(center * center, axis=-1, keepdims=True) + 1e-06)
    return center * inv_std, inv_std


def norm_back(grad_mod, normed, inv_std, scale_row):
    grad_norm = grad_mod * (1.0 + scale_row)
    return inv_std * (
        grad_norm
        - jnp.mean(grad_norm, axis=-1, keepdims=True)
        - normed * jnp.mean(grad_norm * normed, axis=-1, keepdims=True)
    )


def softmax(scores):
    top = jnp.max(scores, axis=-1, keepdims=True)
    raised = jnp.exp(scores - top)
    return raised * (1.0 / jnp.sum(raised, axis=-1, keepdims=True))


def of_head(array, head):
    lane = lax.broadcasted_iota(jnp.int32, array.shape, 1)
    keep = (lane >= head * HEAD_DIM) & (lane < (head + 1) * HEAD_DIM)
    return jnp.where(keep, array, jnp.zeros_like(array))


def pairs(array):
    return array[:, : GW // 2], array[:, GW // 2 :]


def order_matrix(first, rows):
    place = lax.broadcasted_iota(jnp.int32, (rows, 256), 0)
    patch = lax.broadcasted_iota(jnp.int32, (rows, 256), 1)
    return (patch == 4 * (place % ROWS) + first + place // ROWS).astype(F32).astype(BF16)


def chunk_rows(chunk):
    return pl.ds(pl.multiple_of(chunk * ROWS, ROWS), ROWS)


def fetch(sources, buffers, sems):
    copies = [
        pltpu.make_async_copy(source, buffer, sems.at[i])
        for i, (source, buffer) in enumerate(zip(sources, buffers))
    ]
    for copy in copies:
        copy.start()
    return copies


def project(modded, weights):
    joined = nt(modded, weights)
    return tuple(joined[:, i * GW : (i + 1) * GW].astype(BF16) for i in range(3))


def spatial_forward(
    me_ref, x_hbm, w_hbm, ow_hbm, shift_ref, scale_ref,
    p0, p1, p2, p3, qkv_ref, own_ref, x_ref, w_ref, ow_ref, attended_ref, sems,
):
    x_copy, w_copy, ow_copy = fetch(
        (x_hbm, w_hbm.at[0], ow_hbm.at[0]), (x_ref, w_ref, ow_ref), sems
    )
    me = me_ref[0]
    x_copy.wait()
    tokens = x_ref[...]
    normed, _ = normalize(tokens)
    modded = (normed * (1.0 + scale_ref[0:1]) + shift_ref[0:1]).astype(BF16)
    modded = nn(order_matrix(0, 256), modded).astype(BF16)
    own_ref[...] = nn(order_matrix(me, ROWS), tokens).astype(BF16)
    w_copy.wait()
    queries, key_heads, value_heads = project(modded, w_ref[...])
    qkv_ref[0] = queries
    qkv_ref[1] = key_heads
    qkv_ref[2] = value_heads
    attended = []
    for queries_2, keys_2, values_2 in zip(pairs(queries), pairs(key_heads), pairs(value_heads)):
        total = jnp.zeros((256, GW // 2), F32)
        for head in range(2):
            probs = softmax(nt(of_head(queries_2, head), keys_2) * INV_ROOT)
            total = total + nn(probs.astype(BF16), of_head(values_2, head))
        attended.append(total)
    attended = jnp.concatenate(attended, axis=1)
    ow_copy.wait()
    attended_ref[...] = nn(attended.astype(BF16), ow_ref[...]).astype(BF16)
    for k, part in enumerate((p0, p1, p2, p3)):
        part[...] = attended_ref[chunk_rows((me + k) % 4), :]


def temporal(count, me_ref, *refs):
    mids, grads = refs[:count], refs[count : 2 * count]
    w_ref, ow_ref, shift_ref, scale_ref, gate_ref = refs[2 * count : 2 * count + 5]
    part_refs, out_refs = refs[2 * count + 5 : 3 * count + 5], refs[3 * count + 5 :]

    def rows_of(array, i):
        return array[i * ROWS : (i + 1) * ROWS]

    def stack(pieces):
        return jnp.concatenate(pieces, axis=0) if len(pieces) > 1 else pieces[0]

    def spread(array):
        return jnp.concatenate([of_head(array, head) for head in range(HERE)], axis=0)

    def gather_heads(array):
        total = of_head(array[:ROWS], 0)
        for head in range(1, HERE):
            total = total + of_head(rows_of(array, head), head)
        return total

    normed, _ = normalize(stack([ref[...] for ref in mids]))
    modded = (normed * (1.0 + scale_ref[1:2]) + shift_ref[1:2]).astype(BF16)
    grad = stack([ref[...] for ref in grads]).astype(F32)
    grad_proj = (gate_ref[1:2] * grad).astype(BF16)
    queries, key_heads, value_heads = project(modded, w_ref[...])
    grad_attn = nt(grad_proj, ow_ref[...]).astype(BF16)
    joined, attended = [], []
    for i in range(count):
        keys_i, values_i = rows_of(key_heads, i), rows_of(value_heads, i)
        queries_4 = spread(rows_of(queries, i))
        probs = softmax(nt(queries_4, keys_i) * INV_ROOT)
        probs_low = probs.astype(BF16)
        grad_attn_4 = spread(rows_of(grad_attn, i))
        grad_probs = nt(grad_attn_4, values_i)
        grad_scores = (
            probs * (grad_probs - jnp.sum(probs * grad_probs, axis=-1, keepdims=True)) * INV_ROOT
        ).astype(BF16)
        grad_query = gather_heads(nn(grad_scores, keys_i))
        grad_keys = tn(grad_scores, queries_4)
        grad_values = tn(probs_low, grad_attn_4)
        joined.append(
            jnp.concatenate([grad_query, grad_keys, grad_values], axis=1).astype(BF16)
        )
        attended.append(gather_heads(nn(probs_low, values_i)).astype(BF16))
    part = nn(stack(joined), w_ref[...]).astype(BF16)
    out = nn(stack(attended), ow_ref[...]).astype(BF16)
    for i in range(count):
        part_refs[i][...] = rows_of(part, i)
        out_refs[i][...] = rows_of(out, i)


def spatial_backward(
    me_ref, grad_ref, qkv_ref, w_ref, ow_ref, gate_ref, p0, p1, p2, p3, total_ref
):
    grad = jnp.concatenate([grad_ref[chunk] for chunk in range(4)], axis=0)
    grad_proj = (gate_ref[0:1] * grad.astype(F32)).astype(BF16)
    grad_attn = nt(grad_proj, ow_ref[...]).astype(BF16)
    queries, key_heads, value_heads = qkv_ref[0], qkv_ref[1], qkv_ref[2]
    grads = []
    for queries_2, keys_2, values_2, grads_2 in zip(
        pairs(queries), pairs(key_heads), pairs(value_heads), pairs(grad_attn)
    ):
        grad_query = jnp.zeros((256, GW // 2), F32)
        grad_keys, grad_values = grad_query, grad_query
        for head in range(2):
            query = of_head(queries_2, head)
            grad_head = of_head(grads_2, head)
            probs = softmax(nt(query, keys_2) * INV_ROOT)
            grad_probs = nt(grad_head, values_2)
            grad_scores = (
                probs
                * (grad_probs - jnp.sum(probs * grad_probs, axis=-1, keepdims=True))
                * INV_ROOT
            ).astype(BF16)
            grad_query = grad_query + nn(grad_scores, of_head(keys_2, head))
            grad_keys = grad_keys + tn(grad_scores, query)
            grad_values = grad_values + tn(probs.astype(BF16), grad_head)
        grads.append((grad_query, grad_keys, grad_values))
    joined = jnp.concatenate([pair[i] for i in range(3) for pair in grads], axis=1).astype(BF16)
    total_ref[...] = nn(joined, w_ref[...]).astype(BF16)
    for k, part in enumerate((p0, p1, p2, p3)):
        part[...] = total_ref[chunk_rows((me_ref[0] + k) % 4), :]


def add_in(a_ref, b_ref, sum_ref):
    sum_ref[...] = a_ref[...].astype(F32) + b_ref[...].astype(F32)


def put(ref, rows):
    rows = rows.astype(ref.dtype)
    if len(ref.shape) == 3:
        ref[:, 0] = rows[:, : D // 2]
        ref[:, 1] = rows[:, D // 2 :]
    else:
        ref[...] = rows


def block_out(block, x_ref, gate_ref, *refs):
    total = refs[0][...].astype(F32)
    for ref in refs[1:-1]:
        total = total + ref[...].astype(F32)
    put(refs[-1], x_ref[...].astype(F32) + gate_ref[block : block + 1] * total)


def grad_of(block, x_ref, g_ref, scale_ref, *refs):
    total = refs[0][...].astype(F32)
    for ref in refs[1:-1]:
        total = total + ref[...].astype(F32)
    normed, inv_std = normalize(x_ref[...])
    grad = g_ref[...].astype(F32)
    back = norm_back(total, normed, inv_std, scale_ref[block : block + 1])
    put(refs[-1], grad + back)


def pack(grad_ref, result_ref, sent_ref):
    sent_ref[:ROWS] = jnp.concatenate([grad_ref[:, 0], grad_ref[:, 1]], axis=1)
    sent_ref[ROWS:] = result_ref[:HALF]


def pack_last(x_ref, g_ref, scale_ref, early, b3, b2, result_ref, sent_ref):
    grad_of(0, x_ref, g_ref, scale_ref, early, b3, b2, sent_ref.at[:ROWS])
    sent_ref[ROWS:] = result_ref[HALF:]


def unpack(first_ref, last_ref, ends_ref, result_ref, grad_ref):
    stacked = jnp.concatenate([ends_ref[chunk] for chunk in range(4)], axis=0)
    patch = lax.broadcasted_iota(jnp.int32, (256, 256), 0)
    place = lax.broadcasted_iota(jnp.int32, (256, 256), 1)
    order = (patch == 4 * (place % ROWS) + place // ROWS).astype(F32).astype(BF16)
    grad_ref[...] = nn(order, stacked).astype(BF16)
    result_ref[:, :HALF] = first_ref[...]
    result_ref[:, HALF:] = last_ref[...]


IN_HBM = pl.BlockSpec(memory_space=pltpu.HBM)


def whole(shape):
    return pl.BlockSpec(shape, lambda *_: (0,) * len(shape))


QUARTER = whole((ROWS, D))
VECTORS = whole((2, D))
HALVES = jax.ShapeDtypeStruct((ROWS, 2, D // 2), BF16)


def rows_out(dtype=BF16):
    return jax.ShapeDtypeStruct((ROWS, D), dtype)


def run(
    body, me, operands, specs, out_shape, out_specs, flops,
    aliases=None, scratch=(), mib=24, moved=0,
):
    return pl.pallas_call(
        body,
        grid_spec=pltpu.PrefetchScalarGridSpec(
            num_scalar_prefetch=0 if me is None else 1,
            grid=(1,),
            in_specs=specs,
            out_specs=out_specs,
            scratch_shapes=list(scratch),
        ),
        out_shape=out_shape,
        input_output_aliases=aliases or {},
        compiler_params=pltpu.CompilerParams(vmem_limit_bytes=mib * 1024 * 1024),
        cost_estimate=pl.CostEstimate(flops=flops, bytes_accessed=moved, transcendentals=0),
    )(*(() if me is None else (me,)), *operands)


def shift(array, k):
    return lax.ppermute(array, "tp", [(i, (i + k) % N_TP) for i in range(N_TP)])


def across(array):
    return lax.all_to_all(array, "seq", split_axis=0, concat_axis=0, tiled=True)


def weights_of(block, weights, out_weight, after):
    weights, out_weight, _ = lax.optimization_barrier((weights, out_weight, after))
    return weights[block], out_weight[block]


def per_device(tokens, grad_out, qkv_weight, out_weight, mod_shift, mod_scale, mod_gate):
    me = lax.axis_index("tp").astype(jnp.int32).reshape(1)
    tokens = tokens.reshape(256, D)
    weights = jnp.transpose(qkv_weight, (0, 2, 3, 1)).reshape(2, 3 * GW, D)
    qkv_spec = whole((3, 256, GW))

    p0, p1, p2, p3, qkv_s, own = run(
        spatial_forward,
        me,
        (tokens, weights, out_weight, mod_shift, mod_scale),
        [IN_HBM, IN_HBM, IN_HBM, VECTORS, VECTORS],
        (rows_out(),) * 4 + (jax.ShapeDtypeStruct((3, 256, GW), BF16), rows_out()),
        (QUARTER,) * 4 + (qkv_spec, QUARTER),
        1_000_000_000,
        scratch=(
            pltpu.VMEM((256, D), BF16),
            pltpu.VMEM((3 * GW, D), BF16),
            pltpu.VMEM((GW, D), BF16),
            pltpu.VMEM((256, D), BF16),
            pltpu.SemaphoreType.DMA((3,)),
        ),
        mib=58,
    )
    p1, p3, p2 = shift(p1, 1), shift(p3, 3), shift(p2, 2)
    early = run(
        lambda *refs: block_out(0, *refs),
        None, (own, mod_gate, p0, p1), [QUARTER, VECTORS, QUARTER, QUARTER],
        rows_out(F32), QUARTER, 350_000_000,
    )
    middle = run(
        lambda *refs: block_out(0, *refs),
        None, (early, mod_gate, p3, p2), [QUARTER, VECTORS] + [QUARTER] * 2,
        HALVES, whole((ROWS, 2, D // 2)), 1_000_000,
    )
    mid_own = across(middle).reshape(ROWS, D)
    w_spec, ow_spec = whole((3 * GW, D)), whole((GW, D))
    w1, ow1 = weights_of(1, weights, out_weight, mid_own)

    mids = lax.all_gather(mid_own, "tp")
    sent, outs = {}, {}
    for group in GROUPS:
        chunks = [
            pl.BlockSpec((None, ROWS, D), lambda _, at, k=k: ((at[0] + 4 - k) % 4, 0, 0))
            for k in group
        ]
        count = len(group)
        made = run(
            functools.partial(temporal, count), me,
            (mids,) * count + (grad_out,) * count + (w1, ow1, mod_shift, mod_scale, mod_gate),
            chunks * 2 + [w_spec, ow_spec, VECTORS, VECTORS, VECTORS],
            (rows_out(),) * (2 * count), (QUARTER,) * (2 * count),
            50_000_000 if group[-1] else 350_000_000,
        )
        for i, k in enumerate(group):
            sent[k] = shift(made[i], 4 - k) if k else made[i]
            outs[k] = made[count + i]
    total = sent[0]
    for k in (2, 1):
        total = run(
            add_in, None, (total, sent[k]), [QUARTER] * 2, rows_out(F32), QUARTER, 350_000_000
        )
    outs = dict(zip(outs, lax.optimization_barrier(tuple(outs.values()))))
    for k in (2, 1, 3):
        outs[k] = shift(outs[k], 4 - k)
    result_own = run(
        lambda *refs: block_out(1, *refs),
        None, (mid_own, mod_gate, *(outs[k] for k in range(4))),
        [QUARTER, VECTORS] + [QUARTER] * 4, rows_out(), QUARTER, RESULT_FLOPS,
    )

    own_grad = pl.BlockSpec((None, ROWS, D), lambda _, at: (at[0], 0, 0))
    grad_patch = run(
        lambda me_ref, *refs: grad_of(1, *refs),
        me, (mid_own, grad_out, mod_scale, total, sent[3]),
        [QUARTER, own_grad, VECTORS] + [QUARTER] * 2,
        HALVES, whole((ROWS, 2, D // 2)), 1_000_000,
    )
    grad_own = across(grad_patch)
    w0, ow0 = weights_of(0, weights, out_weight, grad_own)
    message = jax.ShapeDtypeStruct((ROWS + HALF, D), BF16)
    packed = run(
        pack, None, (grad_own, result_own), [whole((ROWS, 2, D // 2)), QUARTER],
        message, whole((ROWS + HALF, D)), 1_000_000,
    )
    grads = lax.all_gather(packed, "tp")
    front, back = whole((4, ROWS, D)), pl.BlockSpec((4, HALF, D), lambda *_: (0, 2, 0))
    b0, b1, b2, b3 = run(
        spatial_backward, me, (grads, qkv_s, w0, ow0, mod_gate),
        [front, qkv_spec, w_spec, ow_spec, VECTORS],
        (rows_out(),) * 4, (QUARTER,) * 4, 1_500_000_000,
        scratch=(pltpu.VMEM((256, D), BF16),),
    )
    b1, b3, b2 = shift(b1, 1), shift(b3, 3), shift(b2, 2)
    early = run(add_in, None, (b0, b2), [QUARTER] * 2, rows_out(F32), QUARTER, 350_000_000)
    packed = run(
        pack_last, None, (own, packed, mod_scale, early, b1, b3, result_own),
        [QUARTER] * 2 + [VECTORS] + [QUARTER] * 4,
        message, whole((ROWS + HALF, D)), 1_000_000,
    )
    ends = lax.all_gather(packed, "tp")
    result, grad_in = run(
        unpack, None, (grads, ends, ends), [back, back, front],
        (jax.ShapeDtypeStruct((4, ROWS, D), BF16), jax.ShapeDtypeStruct((256, D), BF16)),
        (whole((4, ROWS, D)), whole((256, D))), 100_000_000,
    )
    return (result, grad_in.reshape(256, 1, D))


def solution(mesh):
    in_specs = (
        P(None, "seq", None),
        P("seq", None, None),
        P(None, None, None, "tp"),
        P(None, "tp", None),
        P(),
        P(),
        P(),
    )
    out_specs = (P("seq", None, None), P(None, "seq", None))
    return jax.shard_map(
        per_device, mesh=mesh, in_specs=in_specs, out_specs=out_specs, check_vma=False
    )
```
